32 devices in a mesh: groups: 2 (over y), leaf: 4 (over z), state: 2 (over x), sub: 2 (over core).
Axes of the slice: x: 2, y: 2, z: 4, core: 2. Of those that a mesh axis runs over, the one named last changes fastest.
Arguments:
- sphere_coef: bfloat16 [12, 25, 2, 2, 4, 2048], P(None, None, None, None, None, ('groups', 'leaf', 'state', 'sub')), parts along dimension 5, may hold values from -6 to 6
- live_blocks: int32 [32], P(('groups', 'leaf', 'state', 'sub')), parts along dimension 0, may hold values from 1 to 4, as said below
- cluster: int32 [2048], P(('groups', 'leaf', 'state', 'sub')), parts along dimension 0, may hold values from 0 to 15
- leaf_parent: int32 [512], P(('groups', 'leaf', 'state', 'sub')), parts along dimension 0, may hold values from 0 to 1
- leaf_octant: int32 [512], P(('groups', 'leaf', 'state', 'sub')), parts along dimension 0, may hold values from 0 to 7
- box_octant: int32 [64], P(('groups', 'leaf', 'state', 'sub')), parts along dimension 0, may hold values from 0 to 7
- rotation: float32 [8, 2, 12, 25, 25], replicated, may hold values from -0.875 to 0.875
- axial_one: float32 [2, 25, 2, 12, 2, 12], replicated, may hold values from -0.3125 to 0.3125
- axial_two: float32 [2, 25, 2, 12, 2, 12], replicated, may hold values from -0.3125 to 0.3125
- owner_rotation: float32 [8, 2, 12, 25, 25], P(('groups', 'leaf')), parts along dimension 0, may hold values from -0.875 to 0.875
- owner_axial: float32 [8, 2, 25, 2, 128, 2, 12], P(('groups', 'leaf'), None, None, None, ('state', 'sub')), parts along dimension 0, may hold values from -0.875 to 0.875
- owner_angle: float32 [8], P('groups'), parts along dimension 0, may hold values from -3.140625 to 3.140625
- turn_table: bfloat16 [8, 128, 25, 256], P(('groups', 'leaf'), ('state', 'sub')), parts along dimension 0, may hold values from -0.625 to 0.625
- angular_table: bfloat16 [256, 128, 32], P('leaf', ('state', 'sub')), may hold values from -0.375 to 0.375
Outputs:
- far_field: float32 [32, 4, 2, 2, 2048], P(('groups', 'leaf', 'state', 'sub')), parts along dimension 0
The draws below stay inside these ranges and needn't reach their ends.
There are 2 independent parts, one for each index of `groups`. The reference program is written for one: setup_inputs(seed, part) draws one part's arguments, and reference() takes and returns one part's arrays. A program takes and returns all parts, laid end to end along the dimension named above; an argument that names none is the same for every part. Nothing has to cross between parts.
Inputs may be any that keep to these rules, and one draw needn't show every extreme that they name: `live_blocks`: live blocks of 16 sphere slots on each device; some device has all 4 live in every draw.
All inputs are finite; a program needn't handle non-finite values.
Results may differ from the reference program's by a relative error of at most 0.018.
Values may be sent and summed in bfloat16 or wider, within the bound.
A program may use at most 64 MiB of HBM per device.

```python
import math
import jax
import jax.numpy as jnp
from jax import lax

L = 12
MW = 25
STATES = 4
SPH_DEV = 64
SBLK = 4
LEAF_DEV = 16
BOX_DEV = 2
PHI = 2048
HOLDERS = 16
SPHERES = 1024
LEAVES = 256
BOXES = 32
NR = 128
MP = 256
THETA = 16
N_LEAF = 4


def draw_live_blocks(key, part):
    first_key, second_key = jax.random.split(key)
    counts = jax.random.randint(first_key, (HOLDERS,), 1, SBLK + 1)
    position = jax.random.randint(second_key, (), 0, HOLDERS)
    return jnp.where(jnp.arange(HOLDERS) == position, SBLK, counts).astype(jnp.int32)


def touch_ends(result, own_key, low, high):
    shape = result.shape
    place = [jax.random.randint(jax.random.fold_in(own_key, axis), (), 0, shape[axis]) for axis in range(len(shape))]
    result = result.at[tuple(place)].set(low)
    longest = shape.index(max(shape))
    place[longest] = (place[longest] + 1) % shape[longest]
    return result.at[tuple(place)].set(high)


def steps_of(own_key, dims, cuts, low, top_value):
    def one(axis_at, parts):
        heights = jax.random.uniform(jax.random.fold_in(jax.random.fold_in(own_key, 6), axis_at), (parts,), jnp.float32, low / len(cuts), top_value / len(cuts))
        return jnp.repeat(jnp.exp(heights), dims[axis_at] // parts).reshape((-1,) + (1,) * (len(dims) - axis_at - 1))

    gain = one(*cuts[0])
    for cut in cuts[1:]:
        gain = gain * one(*cut)
    return gain


def noise(key, dims, deviation, reach, pieces=(), kind=jnp.bfloat16):
    values = deviation * jax.random.normal(key, dims, jnp.float32)
    if pieces:
        values = values * steps_of(key, dims, pieces, -0.22, 0.18)
    return jnp.clip(values, -reach, reach).astype(kind)


def setup_inputs(seed: int = 0, part: int = 0) -> dict:
    seeds = jax.random.split(jax.random.key(seed), 15)
    part_keys = jax.random.split(jax.random.fold_in(seeds[14], part), 15)
    return {
        "sphere_coef": noise(part_keys[0], (L, MW, 2, 2, STATES, SPHERES), 1.0, 6.0, ((5, 16),)),
        "live_blocks": draw_live_blocks(jax.random.fold_in(jax.random.fold_in(seeds[14], part), 71), part),
        "cluster": touch_ends(jax.random.randint(part_keys[2], (SPHERES,), 0, LEAF_DEV), jax.random.fold_in(part_keys[2], 1), 0, LEAF_DEV - 1).astype(jnp.int32),
        "leaf_parent": touch_ends(jax.random.randint(part_keys[3], (LEAVES,), 0, BOX_DEV), jax.random.fold_in(part_keys[3], 1), 0, BOX_DEV - 1).astype(jnp.int32),
        "leaf_octant": touch_ends(jax.random.randint(part_keys[4], (LEAVES,), 0, 8), jax.random.fold_in(part_keys[4], 1), 0, 7).astype(jnp.int32),
        "box_octant": touch_ends(jax.random.randint(part_keys[5], (BOXES,), 0, 8), jax.random.fold_in(part_keys[5], 1), 0, 7).astype(jnp.int32),
        "rotation": noise(seeds[6], (8, 2, L, MW, MW), (2 * MW) ** -0.5, 0.875, (), jnp.float32),
        "axial_one": noise(seeds[7], (2, MW, 2, L, 2, L), (48 * LEAF_DEV // BOX_DEV) ** -0.5, 0.3125, (), jnp.float32),
        "axial_two": noise(seeds[8], (2, MW, 2, L, 2, L), (48 * BOXES // N_LEAF) ** -0.5, 0.3125, (), jnp.float32),
        "owner_rotation": noise(part_keys[9], (N_LEAF, 2, L, MW, MW), (2 * MW) ** -0.5, 0.875, ((0, 4),), jnp.float32),
        "owner_axial": noise(part_keys[10], (N_LEAF, 2, MW, 2, NR, 2, L), 48 ** -0.5, 0.875, ((0, 4), (4, 4)), jnp.float32),
        "owner_angle": jnp.clip(jax.random.uniform(part_keys[11], (N_LEAF,), jnp.float32, -3.140625, 3.140625), -3.140625, 3.140625),
        "turn_table": noise(part_keys[12], (N_LEAF, NR, MW, MP), (MW * N_LEAF) ** -0.5, 0.625, ((0, 4), (1, 4))),
        "angular_table": noise(seeds[13], (MP, NR, 2 * THETA), (2 * NR) ** -0.5, 0.375, ((0, 4), (1, 4))),
    }


def complex_join(first, second, half):
    real = first[..., :half] - second[..., half:]
    imag = first[..., half:] + second[..., :half]
    return jnp.concatenate([real, imag], axis=-1)

def turn_select(vectors, rotation, octants, backward):
    degrees, orders, width = vectors.shape
    if backward:
        mats = jnp.transpose(rotation, (1, 2, 0, 4, 3))
        sign = -1.0
    else:
        mats = jnp.transpose(rotation, (1, 2, 0, 3, 4))
        sign = 1.0
    mats = mats.reshape(2, degrees, 8 * orders, orders)
    first = jnp.einsum('lQp,lpC->lQC', mats[0], vectors, precision=lax.Precision.HIGHEST)
    second = sign * jnp.einsum('lQp,lpC->lQC', mats[1], vectors, precision=lax.Precision.HIGHEST)
    joined = complex_join(first, second, width // 2).reshape(degrees, 8, orders, width)
    count = octants.shape[0]
    chosen = (octants[None, :] == jnp.arange(8, dtype=jnp.int32)[:, None]).astype(jnp.float32)
    column_mask = jnp.tile(chosen, (1, width // count))
    return lax.optimization_barrier(jnp.sum(joined * column_mask[None, :, None, :], axis=1))

def axial_apply(vectors, axial):
    degrees, orders, width = vectors.shape
    rest = width // 4
    moved = vectors.reshape(degrees, orders, 2, 2, rest)
    moved = jnp.transpose(moved, (1, 3, 0, 2, 4)).reshape(orders, 2 * degrees, 2 * rest)
    mats = axial.reshape(2, orders, 2 * degrees, 2 * degrees)
    first = jnp.einsum('qab,qbC->qaC', mats[0], moved, precision=lax.Precision.HIGHEST)
    second = jnp.einsum('qab,qbC->qaC', mats[1], moved, precision=lax.Precision.HIGHEST)
    joined = complex_join(first, second, rest).reshape(orders, 2, degrees, 2, rest)
    return jnp.transpose(joined, (2, 0, 3, 1, 4)).reshape(degrees, orders, width)

def move_expansion(vectors, octants, rotation, axial):
    turned = turn_select(vectors, rotation, octants, False)
    return turn_select(axial_apply(turned, axial), rotation, octants, True)

def local_boxes(sphere_block, live_count, cluster, leaf_parent, leaf_octant, box_octant, rotation, axial_one, axial_two):
    degrees, orders = (sphere_block.shape[0], sphere_block.shape[1])
    channel = sphere_block.shape[2] * sphere_block.shape[3] * sphere_block.shape[4]
    slots = sphere_block.shape[-1]
    per_block = slots // SBLK
    alive = jnp.arange(slots, dtype=jnp.int32) // per_block < live_count
    leaf_total = leaf_parent.shape[0]
    member = ((cluster[:, None] == jnp.arange(leaf_total, dtype=jnp.int32)[None, :]) & alive[:, None]).astype(jnp.float32)
    ident = jnp.eye(channel, dtype=jnp.float32)
    spread = (ident[:, None, :, None] * member[None, :, None, :]).reshape(channel * slots, channel * leaf_total)
    leaves = jnp.dot(sphere_block.reshape(degrees * orders, channel * slots).astype(jnp.float32), spread, precision=lax.Precision.HIGHEST).reshape(degrees, orders, channel * leaf_total)
    moved = move_expansion(leaves, leaf_octant, rotation, axial_one)
    box_total = box_octant.shape[0]
    parents = (leaf_parent[:, None] == jnp.arange(box_total, dtype=jnp.int32)[None, :]).astype(jnp.float32)
    wide_parents = (ident[:, None, :, None] * parents[None, :, None, :]).reshape(channel * leaf_total, channel * box_total)
    boxes = jnp.einsum('lpC,CD->lpD', moved, wide_parents, precision=lax.Precision.HIGHEST)
    outer = move_expansion(boxes, box_octant, rotation, axial_two)
    return outer.reshape(degrees, orders, channel, box_total).sum(-1)

def owner_frame(owner_sum, owner_turn, owner_shift):
    degrees, orders, width = owner_sum.shape
    states = width // 4
    first = jnp.einsum('lqp,lpC->lqC', owner_turn[0], owner_sum, precision=lax.Precision.HIGHEST)
    second = jnp.einsum('lqp,lpC->lqC', owner_turn[1], owner_sum, precision=lax.Precision.HIGHEST)
    turned = complex_join(first, second, width // 2)
    moved = turned.reshape(degrees, orders, 2, 2, states)
    moved = jnp.transpose(moved, (1, 3, 0, 2, 4)).reshape(orders, 2 * degrees, 2 * states)
    root_degrees = owner_shift.shape[3]
    mats = owner_shift.reshape(2, orders, 2 * root_degrees, 2 * degrees)
    first = jnp.einsum('qab,qbC->qaC', mats[0], moved, precision=lax.Precision.HIGHEST)
    second = jnp.einsum('qab,qbC->qaC', mats[1], moved, precision=lax.Precision.HIGHEST)
    joined = complex_join(first, second, states).reshape(orders, 2, root_degrees, 2, states)
    framed = jnp.transpose(joined, (2, 1, 3, 4, 0)).reshape(root_degrees, 4 * states, orders)
    return framed.astype(jnp.bfloat16)

def rotate_back(framed, functions, azimuth, first_order, half_orders):
    root_degrees, width = (framed.shape[0], framed.shape[1])
    states = width // 4
    orders_here = functions.shape[2]
    values = jnp.einsum('nCm,nmj->nCj', framed.astype(jnp.float32), functions.astype(jnp.float32), precision=lax.Precision.HIGHEST)
    values = values.reshape(root_degrees, 2, 2, states, orders_here)
    order_values = (first_order + jnp.arange(orders_here, dtype=jnp.int32) - half_orders).astype(jnp.float32)
    cosine = jnp.cos(order_values * azimuth)
    sine = jnp.sin(order_values * azimuth)
    real_part = cosine * values[:, :, 0] + sine * values[:, :, 1]
    imag_part = cosine * values[:, :, 1] - sine * values[:, :, 0]
    joined = jnp.stack([real_part, imag_part], axis=2)
    return jnp.transpose(joined, (4, 1, 2, 3, 0)).reshape(orders_here, 4 * states * root_degrees)

def legendre_field(root_coef, table):
    orders_here, root_degrees = (table.shape[0], table.shape[1])
    lat_total = table.shape[2] // 2
    rows = root_coef.shape[1] // root_degrees
    states = rows // 4
    half = rows // 2
    blocks = jnp.einsum('jrn,jnK->jrK', root_coef.reshape(orders_here, rows, root_degrees).astype(jnp.float32), table.astype(jnp.float32), precision=lax.Precision.HIGHEST)
    theta_part = blocks[:, :half, :lat_total] + blocks[:, half:, lat_total:]
    cross = blocks[:, :half, lat_total:] + blocks[:, half:, :lat_total]
    phi_part = jnp.concatenate([-cross[:, states:], cross[:, :states]], axis=1)
    return jnp.concatenate([theta_part, phi_part], axis=1)

def phase_table(orders, longitudes):
    order_ids = jnp.arange(orders, dtype=jnp.int32) - orders // 2
    column = jnp.arange(2 * longitudes, dtype=jnp.int32)
    along = column % longitudes
    quarter = (column // longitudes).astype(jnp.float32)
    remainder = jnp.mod(order_ids[:, None] * along[None, :], longitudes)
    phase = remainder.astype(jnp.float32) * (2.0 * math.pi / longitudes) - quarter[None, :] * (0.5 * math.pi)
    return jnp.cos(phase).astype(jnp.bfloat16)

def synthesize(spectrum, longitudes, states):
    orders = spectrum.shape[1]
    table = phase_table(orders, longitudes)
    product = jnp.dot(spectrum.astype(jnp.float32), table.astype(jnp.float32), precision=lax.Precision.HIGHEST)
    product = product.reshape(2, 2, states, -1, 2 * longitudes)
    real_part = product[:, 0, :, :, :longitudes] - product[:, 1, :, :, longitudes:]
    imag_part = product[:, 0, :, :, longitudes:] + product[:, 1, :, :, :longitudes]
    joined = jnp.stack([real_part, imag_part], axis=3)
    return jnp.transpose(joined, (2, 1, 0, 3, 4)) * (1.0 / math.sqrt(orders))

def reference(sphere_coef, live_blocks, cluster, leaf_parent, leaf_octant, box_octant, rotation, axial_one, axial_two, owner_rotation, owner_axial, owner_angle, turn_table, angular_table):
    holders = live_blocks.shape[0]
    grouped = sphere_coef.reshape(sphere_coef.shape[:-1] + (holders, SPH_DEV))
    grouped = jnp.moveaxis(grouped, 5, 0)
    records = (grouped, live_blocks, cluster.reshape(holders, SPH_DEV), leaf_parent.reshape(holders, LEAF_DEV), leaf_octant.reshape(holders, LEAF_DEV), box_octant.reshape(holders, BOX_DEV))

    def one_holder(record):
        return local_boxes(record[0], record[1], record[2], record[3], record[4], record[5], rotation, axial_one, axial_two)
    partials = lax.map(one_holder, records)
    owner_sum = partials.reshape((N_LEAF, holders // N_LEAF) + partials.shape[1:]).sum(axis=1)
    frames = lax.map(lambda record: owner_frame(record[0], record[1], record[2]), (owner_sum, owner_rotation, owner_axial))

    def add_owner(running, record):
        return (running + rotate_back(record[0], record[1], record[2], 0, MP // 2), None)
    initial = jnp.zeros((MP, 16 * NR), jnp.float32)
    root, _ = lax.scan(add_owner, initial, (frames, turn_table, owner_angle))
    root_coef = root.astype(jnp.bfloat16)
    block_rows = MP // N_LEAF

    def synth_block(block_id):
        first_row = block_id * block_rows
        root_piece = lax.dynamic_slice_in_dim(root_coef, first_row, block_rows, 0)
        table_piece = lax.dynamic_slice_in_dim(angular_table, first_row, block_rows, 0)
        return legendre_field(root_piece, table_piece)
    fields = lax.map(synth_block, jnp.arange(N_LEAF, dtype=jnp.int32))
    field_full = fields.reshape(MP, 16, THETA)
    spectrum = jnp.transpose(field_full, (1, 2, 0)).reshape(16 * THETA, MP).astype(jnp.bfloat16)
    return synthesize(spectrum, PHI, STATES)
```

```python
import functools
import math

import jax
import jax.numpy as jnp
from jax import lax
from jax.experimental import pallas as pl
from jax.experimental.pallas import tpu as pltpu
from jax.sharding import PartitionSpec as P

SBLK = 4
PHI = 2048
LP = 16
QP = 32
MESH = pl.DeviceIdType.MESH


def lane_ids():
    lane = lax.broadcasted_iota(jnp.int32, (1, 128), 1)
    return lane, (lane % 64) // 4


def spread_matrix():
    row = lax.broadcasted_iota(jnp.int32, (128, 128), 0)
    col = lax.broadcasted_iota(jnp.int32, (128, 128), 1)
    same = (row // 64 == col // 64) & (row % 4 == col % 4)
    return jnp.where(same, 1.0, 0.0).astype(jnp.bfloat16)


def dot(a, b):
    return jnp.dot(a, b, preferred_element_type=jnp.float32)


def axial_operand(y_ref, q):
    pieces = [y_ref[pl.ds(part * QP + q, LP, stride=2 * QP), :] for part in range(2)]
    here = jnp.concatenate(pieces, axis=0)
    there = pltpu.roll(here, 64, 1)
    return jnp.concatenate([here, there], axis=0).astype(jnp.bfloat16)


def axial_pass(y_ref, z_ref, a_ref, orders):
    lane, _ = lane_ids()
    low = lane < 64
    for q in range(orders):
        r = dot(a_ref[q], axial_operand(y_ref, q))
        z = jnp.where(low, r[: 2 * LP], r[2 * LP :])
        for part in range(2):
            z_ref[pl.ds(part * QP + q, LP, stride=2 * QP), :] = z[part * LP : (part + 1) * LP]


def local_kernel(box_ref, xs_ref, code_ref, f_ref, a1_ref, a2_ref, out_ref, v_ref, y_ref, z_ref):
    degrees = f_ref.shape[0]
    orders = a1_ref.shape[0]
    lane, rep = lane_ids()
    width = 2 * QP
    y_ref[...] = jnp.zeros_like(y_ref)
    z_ref[...] = jnp.zeros_like(z_ref)
    slots = xs_ref.shape[1] // 8
    row = lax.broadcasted_iota(jnp.int32, (8 * slots, 128), 0) // slots
    col = lax.broadcasted_iota(jnp.int32, (8 * slots, 128), 1)
    keep = (
        (row // 4 == col // 64) & (row % 4 == col % 4) & ((col % 64) // 4 == code_ref[...])
    )
    spread = jnp.where(keep, 1.0, 0.0).astype(jnp.bfloat16)
    v_ref[...] = dot(xs_ref[...], spread).astype(jnp.bfloat16)
    octant = rep // 2
    box = rep % 2

    for level in range(2):
        for l in range(degrees):
            v = v_ref[l * width : (l + 1) * width, :]
            if level == 0:
                r = dot(f_ref[l].reshape(8 * width, width), v)
                acc = r[:width]
                for o in range(1, 8):
                    acc = jnp.where(octant == o, r[o * width : (o + 1) * width], acc)
            else:
                acc = dot(f_ref[l, box_ref[0]], v)
                acc = jnp.where(box == 1, dot(f_ref[l, box_ref[1]], v), acc)
            y_ref[l * width : (l + 1) * width, :] = acc
        axial_pass(y_ref, z_ref, a1_ref if level == 0 else a2_ref, orders)
        for l in range(degrees):
            z = z_ref[l * width : (l + 1) * width, :]
            if level == 0:
                mats = f_ref[l].reshape(8 * width, width)
                parts = [jnp.where(octant == o, z, 0.0) for o in range(8)]
            else:
                mats = jnp.concatenate([f_ref[l, box_ref[0]], f_ref[l, box_ref[1]]], axis=0)
                parts = [jnp.where(box == b, z, 0.0) for b in range(2)]
            stacked = jnp.concatenate(parts, axis=0).astype(jnp.bfloat16)
            r = lax.dot_general(
                mats, stacked, (((0,), (0,)), ((), ())), preferred_element_type=jnp.float32
            )
            if level == 0:
                v_ref[l * width : (l + 1) * width, :] = r.astype(jnp.bfloat16)
            else:
                y_ref[l * width : (l + 1) * width, :] = r
    total = degrees * width
    m = y_ref[:total, :]
    hi = m.astype(jnp.bfloat16)
    lo = (m - hi.astype(jnp.float32)).astype(jnp.bfloat16)
    mix = spread_matrix()
    full = dot(hi, mix) + dot(lo, mix)
    rows = total // 16
    packed = full[:rows]
    for r in range(1, 16):
        packed = jnp.where(rep == r, full[r * rows : (r + 1) * rows], packed)
    out_ref[...] = packed


def make_tables(tab_c, tab_s):
    orders = tab_c.shape[0]
    j = lax.broadcasted_iota(jnp.int32, (16, 128), 0) - orders // 2
    k = lax.broadcasted_iota(jnp.int32, (16, 128), 1)
    step = 2.0 * math.pi / PHI
    turns = []
    for a in range(PHI // 128):
        angle = (jnp.bitwise_and(j * (128 * a), PHI - 1)).astype(jnp.float32) * step
        turns.append((jnp.cos(angle), jnp.sin(angle)))

    def body(i, carry):
        r0 = pl.multiple_of(i * 16, 16)
        angle = (jnp.bitwise_and((j + r0) * k, PHI - 1)).astype(jnp.float32) * step
        c1 = jnp.cos(angle)
        s1 = jnp.sin(angle)
        for a, (c2, s2) in enumerate(turns):
            cols = slice(a * 128, (a + 1) * 128)
            tab_c[pl.ds(r0, 16), cols] = (c1 * c2 - s1 * s2).astype(jnp.bfloat16)
            tab_s[pl.ds(r0, 16), cols] = (s1 * c2 + c1 * s2).astype(jnp.bfloat16)
        return carry

    lax.fori_loop(0, orders // 16, body, 0)


def owner_kernel(
    dims,
    packed_ref,
    fo_ref,
    ao_ref,
    cos_ref,
    sin_ref,
    turn_ref,
    ang_ref,
    out_ref,
    recv1,
    y_ref,
    zq_ref,
    vals_ref,
    sbuf,
    recv2,
    root_ref,
    fbuf,
    recv3,
    tab_c,
    tab_s,
    send1,
    rsem1,
    send2,
    rsem2,
    send3,
    rsem3,
):
    leaf_size, state_size, sub_size = dims
    group = state_size * sub_size
    holders = leaf_size * group
    my_groups = lax.axis_index("groups")
    my_leaf = lax.axis_index("leaf")
    my_state = lax.axis_index("state")
    my_sub = lax.axis_index("sub")
    my_g = my_state * sub_size + my_sub
    me = my_leaf * group + my_g
    degrees = fo_ref.shape[0]
    q_orders = ao_ref.shape[0]
    nloc = turn_ref.shape[0]
    orders = turn_ref.shape[2]
    width = 2 * QP
    lane, rep = lane_ids()
    low = lane < 64

    def device(index):
        g = lax.rem(index, group)
        return (my_groups, index // group, g // sub_size, lax.rem(g, sub_size))

    barrier = pltpu.get_barrier_semaphore()

    def greet(d, carry):
        pl.semaphore_signal(
            barrier, inc=1, device_id=device(lax.rem(me + d, holders)), device_id_type=MESH
        )
        return carry

    lax.fori_loop(1, holders, greet, 0)
    pl.semaphore_wait(barrier, holders - 1)

    copies = []
    for d in range(1, group):
        target = my_leaf * group + lax.rem(my_g + d, group)
        copy = pltpu.make_async_remote_copy(
            src_ref=packed_ref,
            dst_ref=recv1.at[d - 1],
            send_sem=send1.at[d - 1],
            recv_sem=rsem1.at[d - 1],
            device_id=device(target),
            device_id_type=MESH,
        )
        copy.start()
        copies.append(copy)

    y_ref[...] = jnp.zeros_like(y_ref)
    zq_ref[...] = jnp.zeros_like(zq_ref)
    make_tables(tab_c, tab_s)

    for copy in copies:
        copy.wait()
    packed = packed_ref[...]
    for d in range(1, group):
        packed = packed + recv1[d - 1]
    parts = [jnp.where(rep == r, packed, 0.0) for r in range(16)]
    vectors = dot(
        jnp.concatenate(parts, axis=0).astype(jnp.bfloat16), spread_matrix()
    ).astype(jnp.bfloat16)
    for l in range(degrees):
        y_ref[l * width : (l + 1) * width, :] = dot(
            fo_ref[l], vectors[l * width : (l + 1) * width]
        )
    for q in range(q_orders):
        r = dot(ao_ref[q], axial_operand(y_ref, q))
        zq_ref[q * 2 * nloc : (q + 1) * 2 * nloc, :] = jnp.where(
            low, r[: 2 * nloc], r[2 * nloc :]
        )

    cosine = cos_ref[...]
    sine = sin_ref[...]
    for block in range(nloc // 8):
        gathered = jnp.zeros((QP, 128), jnp.float32)
        for n8 in range(8):
            n = block * 8 + n8
            real = zq_ref[pl.ds(n, QP, stride=2 * nloc), :]
            imag = zq_ref[pl.ds(nloc + n, QP, stride=2 * nloc), :]
            both = jnp.where(rep % 2 == 0, real, imag)
            gathered = jnp.where(rep // 2 == n8, both, gathered)
        flipped = gathered.T
        for n8 in range(8):
            n = block * 8 + n8
            framed = jnp.concatenate(
                [flipped[n8 * 8 : n8 * 8 + 8], flipped[64 + n8 * 8 : 72 + n8 * 8]], axis=0
            ).astype(jnp.bfloat16)
            values = dot(framed, turn_ref[n])
            for u in range(2):
                v = values[u * 8 : u * 8 + 8]
                vals_ref[n, u * 8 : u * 8 + 8, :] = cosine * v + sine * pltpu.roll(v, 4, 0)

    half = nloc // 2
    for m in range(orders // 128):
        cols = slice(m * 128, (m + 1) * 128)
        for n in range(half):
            a = vals_ref[n, :, cols]
            b = vals_ref[n + half, :, cols]
            rows = slice(n * 16, (n + 1) * 16)
            sbuf[2 * m, rows, :] = jnp.where(low, a, pltpu.roll(b, 64, 1)).astype(jnp.bfloat16)
            sbuf[2 * m + 1, rows, :] = jnp.where(low, pltpu.roll(a, 64, 1), b).astype(
                jnp.bfloat16
            )

    copies = []
    for d in range(1, leaf_size):
        to_leaf = lax.rem(my_leaf + d, leaf_size)
        copy = pltpu.make_async_remote_copy(
            src_ref=sbuf.at[to_leaf],
            dst_ref=recv2.at[d - 1],
            send_sem=send2.at[d - 1],
            recv_sem=rsem2.at[d - 1],
            device_id=device(to_leaf * group + my_g),
            device_id_type=MESH,
        )
        copy.start()
        copies.append(copy)
    for copy in copies:
        copy.wait()
    root = sbuf[my_leaf].astype(jnp.float32)
    for d in range(1, leaf_size):
        root = root + recv2[d - 1].astype(jnp.float32)
    root_ref[...] = root.astype(jnp.bfloat16).astype(jnp.float32)

    lats = ang_ref.shape[1] // 2
    sign = jnp.where(lax.broadcasted_iota(jnp.int32, (8, 128), 0) < 4, -1.0, 1.0)

    def latitude(h, carry):
        theta = jnp.zeros((8, 128), jnp.float32)
        cross = jnp.zeros((8, 128), jnp.float32)
        for n in range(half):
            a0 = ang_ref[n, pl.ds(h, 1), :]
            a1 = ang_ref[n, pl.ds(lats + h, 1), :]
            r0 = root_ref[n * 16 : n * 16 + 8, :]
            r1 = root_ref[n * 16 + 8 : n * 16 + 16, :]
            theta = theta + (a0 * r0 + a1 * r1)
            cross = cross + (a1 * r0 + a0 * r1)
        theta = theta + pltpu.roll(theta, 64, 1)
        cross = cross + pltpu.roll(cross, 64, 1)
        phi = sign * pltpu.roll(cross, 4, 0)
        fbuf[h] = jnp.concatenate([theta, phi], axis=0).astype(jnp.bfloat16)
        return carry

    lax.fori_loop(0, lats, latitude, 0)

    def field_copy(d):
        target = lax.rem(me + d, holders)
        return pltpu.make_async_remote_copy(
            src_ref=fbuf.at[target],
            dst_ref=recv3.at[me],
            send_sem=send3.at[d - 1],
            recv_sem=rsem3.at[d - 1],
            device_id=device(target),
            device_id_type=MESH,
        )

    def start(d, carry):
        field_copy(d).start()
        return carry

    def finish(d, carry):
        field_copy(d).wait_send()
        source = lax.rem(me + holders - d, holders)
        pltpu.make_async_remote_copy(
            src_ref=fbuf.at[source],
            dst_ref=recv3.at[source],
            send_sem=send3.at[d - 1],
            recv_sem=rsem3.at[d - 1],
            device_id=device(source),
            device_id_type=MESH,
        ).wait_recv()
        return carry

    lax.fori_loop(1, holders, start, 0)
    recv3[me] = fbuf[me]
    lax.fori_loop(1, holders, finish, 0)

    pieces = []
    for leaf in range(leaf_size):
        total = recv3[leaf * group].astype(jnp.float32)
        for g in range(1, group):
            total = total + recv3[leaf * group + g].astype(jnp.float32)
        pieces.append(total)
    spectrum = jnp.concatenate(
        [
            jnp.where(low, pieces[2 * m], pieces[2 * m + 1]).astype(jnp.bfloat16)
            for m in range(leaf_size // 2)
        ],
        axis=1,
    )
    scale = 1.0 / math.sqrt(orders)
    for tile in range(PHI // 512):
        cols = slice(tile * 512, (tile + 1) * 512)
        first = dot(spectrum, tab_c[:, cols])
        second = dot(spectrum, tab_s[:, cols])
        for c in range(2):
            rows = slice(c * 8, c * 8 + 8)
            turned = pltpu.roll(second[rows], 4, 0)
            out_ref[rows, cols] = (first[rows] + jnp.tile(sign, (1, 4)) * turned) * scale


def pad_last(x, *sizes):
    skip = x.ndim - len(sizes)
    return jnp.pad(
        x, [(0, 0)] * skip + [(0, s - n) for s, n in zip(sizes, x.shape[skip:], strict=True)]
    )


def rotation_blocks(real, imag):
    real = pad_last(real.astype(jnp.bfloat16), QP, QP)
    imag = pad_last(imag.astype(jnp.bfloat16), QP, QP)
    return jnp.concatenate(
        [jnp.concatenate([real, -imag], -1), jnp.concatenate([imag, real], -1)], -2
    )


def axial_blocks(axial, out_rows):
    mats = axial.astype(jnp.bfloat16)
    mats = jnp.stack([mats[:, :, 0], mats[:, :, 1, :, ::-1]], axis=2)
    mats = jnp.transpose(mats, (0, 1, 2, 4, 3, 5))
    mats = pad_last(mats, out_rows, LP)
    real, imag = mats[0], mats[1]
    blocks = jnp.stack([jnp.stack([real, -imag], 0), jnp.stack([imag, real], 0)], 0)
    blocks = jnp.transpose(blocks, (2, 3, 0, 5, 4, 1, 6))
    orders = axial.shape[1]
    return blocks.reshape(orders, 4 * out_rows, 4 * LP)


def on_device(
    dims,
    sphere_coef,
    live_blocks,
    cluster,
    leaf_parent,
    leaf_octant,
    box_octant,
    rotation,
    axial_one,
    axial_two,
    owner_rotation,
    owner_axial,
    owner_angle,
    turn_table,
    angular_table,
):
    leaf_size, state_size, sub_size = dims
    group = state_size * sub_size
    holders = leaf_size * group
    degrees, morders = sphere_coef.shape[:2]
    slots = sphere_coef.shape[-1]
    bf16 = jnp.bfloat16
    f32 = jnp.float32

    leaf_code = leaf_octant * 2 + leaf_parent
    member = cluster[:, None] == jnp.arange(leaf_code.shape[0], dtype=jnp.int32)[None, :]
    code = jnp.sum(jnp.where(member, leaf_code[None, :], 0), axis=1)
    alive = jnp.arange(slots, dtype=jnp.int32) // (slots // SBLK) < live_blocks[0]
    code = jnp.where(alive, code, -1)
    code = jnp.broadcast_to(code[None, :], (8, slots)).reshape(8 * slots, 1)

    xs = jnp.transpose(sphere_coef, (0, 2, 1, 3, 4, 5)).reshape(degrees, 2, morders, 8 * slots)
    xs = pad_last(xs, QP, 8 * slots).reshape(degrees * 2 * QP, 8 * slots)
    turns = jnp.transpose(rotation, (1, 2, 0, 3, 4))
    f = rotation_blocks(turns[0], turns[1])
    a1 = axial_blocks(axial_one, LP)
    a2 = axial_blocks(axial_two, LP)
    rows = degrees * 2 * QP
    vmem = pl.BlockSpec(memory_space=pltpu.VMEM)
    packed = pl.pallas_call(
        local_kernel,
        out_shape=jax.ShapeDtypeStruct((rows // 16, 128), f32),
        in_specs=[pl.BlockSpec(memory_space=pltpu.SMEM)] + [vmem] * 5,
        out_specs=vmem,
        scratch_shapes=[
            pltpu.VMEM((rows, 128), bf16),
            pltpu.VMEM((LP * 2 * QP, 128), f32),
            pltpu.VMEM((LP * 2 * QP, 128), f32),
        ],
        compiler_params=pltpu.CompilerParams(vmem_limit_bytes=32 * 1024 * 1024),
    )(box_octant, xs, code, f, a1, a2)

    fo = rotation_blocks(owner_rotation[0, 0], owner_rotation[0, 1])
    nloc = turn_table.shape[1]
    orders = turn_table.shape[3]
    ao = axial_blocks(owner_axial[0], nloc)
    azimuth = owner_angle[lax.axis_index("leaf")]
    order_values = (jnp.arange(orders, dtype=jnp.int32) - orders // 2).astype(f32)
    flip = jnp.where(jnp.arange(8) < 4, 1.0, -1.0).astype(f32)
    cosine = jnp.broadcast_to(jnp.cos(order_values * azimuth)[None, :], (8, orders))
    sine = flip[:, None] * jnp.sin(order_values * azimuth)[None, :]
    turn = pad_last(turn_table[0], QP, orders)
    own = angular_table.shape[0]
    ang = jnp.transpose(angular_table, (1, 2, 0)).reshape(2, nloc // 2, -1, own)
    ang = jnp.concatenate([ang[0], ang[1]], axis=-1).astype(f32)
    lats = ang.shape[1] // 2
    assert own == 64 and lats == holders and orders == 64 * leaf_size

    out = pl.pallas_call(
        functools.partial(owner_kernel, dims),
        out_shape=jax.ShapeDtypeStruct((16, PHI), f32),
        in_specs=[vmem] * 7,
        out_specs=vmem,
        scratch_shapes=[
            pltpu.VMEM((group - 1, rows // 16, 128), f32),
            pltpu.VMEM((LP * 2 * QP, 128), f32),
            pltpu.VMEM((QP * 2 * nloc, 128), f32),
            pltpu.VMEM((nloc, 16, orders), f32),
            pltpu.VMEM((leaf_size, 8 * nloc, 128), bf16),
            pltpu.VMEM((leaf_size - 1, 8 * nloc, 128), bf16),
            pltpu.VMEM((8 * nloc, 128), f32),
            pltpu.VMEM((lats, 16, 128), bf16),
            pltpu.VMEM((holders, 16, 128), bf16),
            pltpu.VMEM((orders, PHI), bf16),
            pltpu.VMEM((orders, PHI), bf16),
            pltpu.SemaphoreType.DMA((group - 1,)),
            pltpu.SemaphoreType.DMA((group - 1,)),
            pltpu.SemaphoreType.DMA((leaf_size - 1,)),
            pltpu.SemaphoreType.DMA((leaf_size - 1,)),
            pltpu.SemaphoreType.DMA((holders - 1,)),
            pltpu.SemaphoreType.DMA((holders - 1,)),
        ],
        compiler_params=pltpu.CompilerParams(
            collective_id=0, has_side_effects=True, vmem_limit_bytes=48 * 1024 * 1024
        ),
    )(packed, fo, ao, cosine, sine, turn, ang)
    out = out.reshape(2, 2, 4, PHI)
    return jnp.transpose(out, (2, 0, 1, 3))[None]


def solution(mesh):
    dims = (mesh.shape["leaf"], mesh.shape["state"], mesh.shape["sub"])
    split = ("groups", "leaf", "state", "sub")
    return jax.shard_map(
        functools.partial(on_device, dims),
        mesh=mesh,
        in_specs=(
            P(None, None, None, None, None, split),
            P(split),
            P(split),
            P(split),
            P(split),
            P(split),
            P(),
            P(),
            P(),
            P(("groups", "leaf"), None, None, None, None),
            P(("groups", "leaf"), None, None, None, ("state", "sub"), None, None),
            P("groups"),
            P(("groups", "leaf"), ("state", "sub"), None, None),
            P("leaf", ("state", "sub"), None),
        ),
        out_specs=P(split, None, None, None, None),
        check_vma=False,
    )
```

```python
import functools
import math

import jax
import jax.numpy as jnp
from jax import lax
from jax.experimental import pallas as pl
from jax.experimental.pallas import tpu as pltpu
from jax.sharding import PartitionSpec as P

SBLK = 4
PHI = 2048
LP = 16
QP = 32
MESH = pl.DeviceIdType.MESH


def lane_ids():
    lane = lax.broadcasted_iota(jnp.int32, (1, 128), 1)
    return lane, (lane % 64) // 4


def spread_matrix():
    row = lax.broadcasted_iota(jnp.int32, (128, 128), 0)
    col = lax.broadcasted_iota(jnp.int32, (128, 128), 1)
    same = (row // 64 == col // 64) & (row % 4 == col % 4)
    return jnp.where(same, 1.0, 0.0).astype(jnp.bfloat16)


def dot(a, b):
    return jnp.dot(a, b, preferred_element_type=jnp.float32)


def axial_operand(y_ref, q):
    lane, _ = lane_ids()
    low = lane < 64
    real, imag = [y_ref[pl.ds(part * QP + q, LP, stride=2 * QP), :] for part in range(2)]
    real_turned = pltpu.roll(real, 64, 1)
    imag_turned = pltpu.roll(imag, 64, 1)
    return jnp.concatenate(
        [
            jnp.where(low, real, imag_turned),
            jnp.where(low, real_turned, imag),
            jnp.where(low, -imag, real_turned),
            jnp.where(low, -imag_turned, real),
        ],
        axis=0,
    ).astype(jnp.bfloat16)


def axial_result(r):
    lane, _ = lane_ids()
    low = lane < 64
    half = r.shape[0] // 2
    first, second = r[:half], r[half:]
    real = jnp.where(low, first, pltpu.roll(second, 64, 1))
    imag = jnp.where(low, pltpu.roll(first, 64, 1), second)
    return real, imag


def identity(rows):
    row = lax.broadcasted_iota(jnp.int32, (rows, 128), 0)
    col = lax.broadcasted_iota(jnp.int32, (rows, 128), 1)
    return jnp.where(row == col, 1.0, 0.0).astype(jnp.bfloat16)


def dot_nt(a, b):
    return lax.dot_general(a, b, (((1,), (1,)), ((), ())), preferred_element_type=jnp.float32)


def axial_matrices(s_ref, a_ref, degrees):
    eye = identity(QP)
    zeros = jnp.zeros((64, 128), jnp.float32)
    for u in range(2):
        for w in range(degrees):
            pieces = []
            for part in range(2):
                base = ((part * 2 + u) * degrees + w) * degrees * 2
                for t in range(2):
                    pieces.append(s_ref[pl.ds(base + t, LP, stride=2), :])
            block = jnp.concatenate(pieces + [zeros], axis=0).astype(jnp.bfloat16)
            a_ref[pl.ds(u * LP + w, QP, stride=2 * LP), :] = dot_nt(eye, block)


def axial_pass(y_ref, z_ref, a_ref, orders):
    for q in range(orders):
        mats = a_ref[q * 2 * LP : (q + 1) * 2 * LP, :][:, :64].astype(jnp.bfloat16)
        for part, z in enumerate(axial_result(dot(mats, axial_operand(y_ref, q)))):
            z_ref[pl.ds(part * QP + q, LP, stride=2 * QP), :] = z


def local_kernel(
    orders, box_ref, xs_ref, code_ref, f_ref, s1_ref, s2_ref, out_ref, v_ref, y_ref, z_ref, a1_ref, a2_ref
):
    degrees = f_ref.shape[0]
    for s_ref, a_ref in ((s1_ref, a1_ref), (s2_ref, a2_ref)):
        a_ref[...] = jnp.zeros_like(a_ref)
        axial_matrices(s_ref, a_ref, degrees)
    lane, rep = lane_ids()
    width = 2 * QP
    y_ref[...] = jnp.zeros_like(y_ref)
    z_ref[...] = jnp.zeros_like(z_ref)
    slots = xs_ref.shape[1] // 8
    row = lax.broadcasted_iota(jnp.int32, (8 * slots, 128), 0) // slots
    col = lax.broadcasted_iota(jnp.int32, (8 * slots, 128), 1)
    keep = (
        (row // 4 == col // 64) & (row % 4 == col % 4) & ((col % 64) // 4 == code_ref[...])
    )
    spread = jnp.where(keep, 1.0, 0.0).astype(jnp.bfloat16)
    v_ref[...] = dot(xs_ref[...], spread).astype(jnp.bfloat16)
    octant = rep // 2
    box = rep % 2

    for level in range(2):
        for l in range(degrees):
            v = v_ref[l * width : (l + 1) * width, :]
            if level == 0:
                r = dot(f_ref[l].reshape(8 * width, width), v)
                acc = r[:width]
                for o in range(1, 8):
                    acc = jnp.where(octant == o, r[o * width : (o + 1) * width], acc)
            else:
                acc = dot(f_ref[l, box_ref[0]], v)
                acc = jnp.where(box == 1, dot(f_ref[l, box_ref[1]], v), acc)
            y_ref[l * width : (l + 1) * width, :] = acc
        axial_pass(y_ref, z_ref, a1_ref if level == 0 else a2_ref, orders)
        for l in range(degrees):
            z = z_ref[l * width : (l + 1) * width, :]
            if level == 0:
                mats = f_ref[l].reshape(8 * width, width)
                parts = [jnp.where(octant == o, z, 0.0) for o in range(8)]
            else:
                mats = jnp.concatenate([f_ref[l, box_ref[0]], f_ref[l, box_ref[1]]], axis=0)
                parts = [jnp.where(box == b, z, 0.0) for b in range(2)]
            stacked = jnp.concatenate(parts, axis=0).astype(jnp.bfloat16)
            r = lax.dot_general(
                mats, stacked, (((0,), (0,)), ((), ())), preferred_element_type=jnp.float32
            )
            if level == 0:
                v_ref[l * width : (l + 1) * width, :] = r.astype(jnp.bfloat16)
            else:
                y_ref[l * width : (l + 1) * width, :] = r
    total = degrees * width
    m = y_ref[:total, :]
    hi = m.astype(jnp.bfloat16)
    lo = (m - hi.astype(jnp.float32)).astype(jnp.bfloat16)
    mix = spread_matrix()
    full = dot(hi, mix) + dot(lo, mix)
    rows = total // 16
    packed = full[:rows]
    for r in range(1, 16):
        packed = jnp.where(rep == r, full[r * rows : (r + 1) * rows], packed)
    out_ref[...] = packed


def make_tables(tab_c, tab_s):
    orders = tab_c.shape[0]
    j = lax.broadcasted_iota(jnp.int32, (16, 128), 0) - orders // 2
    k = lax.broadcasted_iota(jnp.int32, (16, 128), 1)
    step = 2.0 * math.pi / PHI
    turns = []
    for a in range(PHI // 128):
        angle = (jnp.bitwise_and(j * (128 * a), PHI - 1)).astype(jnp.float32) * step
        turns.append((jnp.cos(angle), jnp.sin(angle)))

    def body(i, carry):
        r0 = pl.multiple_of(i * 16, 16)
        angle = (jnp.bitwise_and((j + r0) * k, PHI - 1)).astype(jnp.float32) * step
        c1 = jnp.cos(angle)
        s1 = jnp.sin(angle)
        for a, (c2, s2) in enumerate(turns):
            cols = slice(a * 128, (a + 1) * 128)
            tab_c[pl.ds(r0, 16), cols] = (c1 * c2 - s1 * s2).astype(jnp.bfloat16)
            tab_s[pl.ds(r0, 16), cols] = (s1 * c2 + c1 * s2).astype(jnp.bfloat16)
        return carry

    lax.fori_loop(0, orders // 16, body, 0)


def owner_kernel(
    dims,
    packed_ref,
    fo_ref,
    so_ref,
    angle_ref,
    turn_ref,
    ang_ref,
    out_ref,
    recv1,
    ao_ref,
    y_ref,
    zq_ref,
    vals_ref,
    sbuf,
    recv2,
    root_ref,
    fbuf,
    recv3,
    tab_c,
    tab_s,
    send1,
    rsem1,
    send2,
    rsem2,
    send3,
    rsem3,
):
    leaf_size, state_size, sub_size = dims
    group = state_size * sub_size
    holders = leaf_size * group
    my_groups = lax.axis_index("groups")
    my_leaf = lax.axis_index("leaf")
    my_state = lax.axis_index("state")
    my_sub = lax.axis_index("sub")
    my_g = my_state * sub_size + my_sub
    me = my_leaf * group + my_g
    degrees = fo_ref.shape[0]
    q_orders = ao_ref.shape[0]
    nloc = turn_ref.shape[0]
    orders = turn_ref.shape[2]
    width = 2 * QP
    lane, rep = lane_ids()
    low = lane < 64

    def device(index):
        g = lax.rem(index, group)
        return (my_groups, index // group, g // sub_size, lax.rem(g, sub_size))

    barrier = pltpu.get_barrier_semaphore()

    def greet(d, carry):
        pl.semaphore_signal(
            barrier, inc=1, device_id=device(lax.rem(me + d, holders)), device_id_type=MESH
        )
        return carry

    lax.fori_loop(1, holders, greet, 0)
    pl.semaphore_wait(barrier, holders - 1)

    copies = []
    for d in range(1, group):
        target = my_leaf * group + lax.rem(my_g + d, group)
        copy = pltpu.make_async_remote_copy(
            src_ref=packed_ref,
            dst_ref=recv1.at[d - 1],
            send_sem=send1.at[d - 1],
            recv_sem=rsem1.at[d - 1],
            device_id=device(target),
            device_id_type=MESH,
        )
        copy.start()
        copies.append(copy)

    y_ref[...] = jnp.zeros_like(y_ref)
    zq_ref[...] = jnp.zeros_like(zq_ref)
    eye = identity(2 * nloc)
    for q in range(q_orders):
        pieces = []
        for part in range(2):
            for t in range(2):
                first, second = [
                    so_ref[
                        pl.ds(((part * q_orders + q) * 2 + u) * degrees * 2 + t, LP, stride=2), :
                    ]
                    for u in range(2)
                ]
                pieces.append(first + pltpu.roll(second, nloc, 1))
        ao_ref[q] = dot_nt(eye, jnp.concatenate(pieces, axis=0).astype(jnp.bfloat16)).astype(
            jnp.bfloat16
        )
    azimuth = angle_ref[my_leaf]
    order_values = (
        lax.broadcasted_iota(jnp.int32, (8, orders), 1) - orders // 2
    ).astype(jnp.float32)
    cosine = jnp.cos(order_values * azimuth)
    sine = jnp.sin(order_values * azimuth)
    sine = jnp.where(lax.broadcasted_iota(jnp.int32, (8, orders), 0) < 4, sine, -sine)

    for copy in copies:
        copy.wait()
    packed = packed_ref[...]
    for d in range(1, group):
        packed = packed + recv1[d - 1]
    parts = [jnp.where(rep == r, packed, 0.0) for r in range(16)]
    vectors = dot(
        jnp.concatenate(parts, axis=0).astype(jnp.bfloat16), spread_matrix()
    ).astype(jnp.bfloat16)
    for l in range(degrees):
        y_ref[l * width : (l + 1) * width, :] = dot(
            fo_ref[l], vectors[l * width : (l + 1) * width]
        )
    for q in range(q_orders):
        for part, z in enumerate(axial_result(dot(ao_ref[q], axial_operand(y_ref, q)))):
            start = (q * 2 + part) * nloc
            zq_ref[start : start + nloc, :] = z

    for block in range(nloc // 8):
        gathered = jnp.zeros((QP, 128), jnp.float32)
        for n8 in range(8):
            n = block * 8 + n8
            real = zq_ref[pl.ds(n, QP, stride=2 * nloc), :]
            imag = zq_ref[pl.ds(nloc + n, QP, stride=2 * nloc), :]
            both = jnp.where(rep % 2 == 0, real, imag)
            gathered = jnp.where(rep // 2 == n8, both, gathered)
        flipped = gathered.T
        for n8 in range(8):
            n = block * 8 + n8
            framed = jnp.concatenate(
                [flipped[n8 * 8 : n8 * 8 + 8], flipped[64 + n8 * 8 : 72 + n8 * 8]], axis=0
            ).astype(jnp.bfloat16)
            values = dot(framed, turn_ref[n])
            for u in range(2):
                v = values[u * 8 : u * 8 + 8]
                vals_ref[n, u * 8 : u * 8 + 8, :] = cosine * v + sine * pltpu.roll(v, 4, 0)

    half = nloc // 2
    for m in range(orders // 128):
        cols = slice(m * 128, (m + 1) * 128)
        for n in range(half):
            a = vals_ref[n, :, cols]
            b = vals_ref[n + half, :, cols]
            rows = slice(n * 16, (n + 1) * 16)
            sbuf[2 * m, rows, :] = jnp.where(low, a, pltpu.roll(b, 64, 1)).astype(jnp.bfloat16)
            sbuf[2 * m + 1, rows, :] = jnp.where(low, pltpu.roll(a, 64, 1), b).astype(
                jnp.bfloat16
            )

    copies = []
    for d in range(1, leaf_size):
        to_leaf = lax.rem(my_leaf + d, leaf_size)
        copy = pltpu.make_async_remote_copy(
            src_ref=sbuf.at[to_leaf],
            dst_ref=recv2.at[d - 1],
            send_sem=send2.at[d - 1],
            recv_sem=rsem2.at[d - 1],
            device_id=device(to_leaf * group + my_g),
            device_id_type=MESH,
        )
        copy.start()
        copies.append(copy)
    make_tables(tab_c, tab_s)
    for copy in copies:
        copy.wait()
    root = sbuf[my_leaf].astype(jnp.float32)
    for d in range(1, leaf_size):
        root = root + recv2[d - 1].astype(jnp.float32)
    root_ref[...] = root.astype(jnp.bfloat16).astype(jnp.float32)

    lats = ang_ref.shape[1] // 2
    sign = jnp.where(lax.broadcasted_iota(jnp.int32, (8, 128), 0) < 4, -1.0, 1.0)

    def latitude(h, carry):
        theta = jnp.zeros((8, 128), jnp.float32)
        cross = jnp.zeros((8, 128), jnp.float32)
        for n in range(half):
            a0 = ang_ref[n, pl.ds(h, 1), :]
            a1 = ang_ref[n, pl.ds(lats + h, 1), :]
            r0 = root_ref[n * 16 : n * 16 + 8, :]
            r1 = root_ref[n * 16 + 8 : n * 16 + 16, :]
            theta = theta + (a0 * r0 + a1 * r1)
            cross = cross + (a1 * r0 + a0 * r1)
        theta = theta + pltpu.roll(theta, 64, 1)
        cross = cross + pltpu.roll(cross, 64, 1)
        phi = sign * pltpu.roll(cross, 4, 0)
        fbuf[h] = jnp.concatenate([theta, phi], axis=0).astype(jnp.bfloat16)
        return carry

    lax.fori_loop(0, lats, latitude, 0)

    def field_copy(d):
        target = lax.rem(me + d, holders)
        return pltpu.make_async_remote_copy(
            src_ref=fbuf.at[target],
            dst_ref=recv3.at[me],
            send_sem=send3.at[d - 1],
            recv_sem=rsem3.at[d - 1],
            device_id=device(target),
            device_id_type=MESH,
        )

    def start(d, carry):
        field_copy(d).start()
        return carry

    def finish(d, carry):
        field_copy(d).wait_send()
        source = lax.rem(me + holders - d, holders)
        pltpu.make_async_remote_copy(
            src_ref=fbuf.at[source],
            dst_ref=recv3.at[source],
            send_sem=send3.at[d - 1],
            recv_sem=rsem3.at[d - 1],
            device_id=device(source),
            device_id_type=MESH,
        ).wait_recv()
        return carry

    lax.fori_loop(1, holders, start, 0)
    recv3[me] = fbuf[me]
    lax.fori_loop(1, holders, finish, 0)

    pieces = []
    for leaf in range(leaf_size):
        total = recv3[leaf * group].astype(jnp.float32)
        for g in range(1, group):
            total = total + recv3[leaf * group + g].astype(jnp.float32)
        pieces.append(total)
    spectrum = jnp.concatenate(
        [
            jnp.where(low, pieces[2 * m], pieces[2 * m + 1]).astype(jnp.bfloat16)
            for m in range(leaf_size // 2)
        ],
        axis=1,
    )
    scale = 1.0 / math.sqrt(orders)
    for tile in range(PHI // 512):
        cols = slice(tile * 512, (tile + 1) * 512)
        first = dot(spectrum, tab_c[:, cols])
        second = dot(spectrum, tab_s[:, cols])
        for c in range(2):
            rows = slice(c * 8, c * 8 + 8)
            turned = pltpu.roll(second[rows], 4, 0)
            out_ref[rows, cols] = (first[rows] + jnp.tile(sign, (1, 4)) * turned) * scale


def pad_last(x, *sizes):
    skip = x.ndim - len(sizes)
    return jnp.pad(
        x, [(0, 0)] * skip + [(0, s - n) for s, n in zip(sizes, x.shape[skip:], strict=True)]
    )


def rotation_blocks(real, imag):
    real = pad_last(real.astype(jnp.bfloat16), QP, QP)
    imag = pad_last(imag.astype(jnp.bfloat16), QP, QP)
    return jnp.concatenate(
        [jnp.concatenate([real, -imag], -1), jnp.concatenate([imag, real], -1)], -2
    )


def axial_rows(mats):
    mats = mats.reshape(-1, mats.shape[-1])
    return jnp.pad(mats, ((0, 16), (0, 128 - mats.shape[1])))


def on_device(
    dims,
    sphere_coef,
    live_blocks,
    cluster,
    leaf_parent,
    leaf_octant,
    box_octant,
    rotation,
    axial_one,
    axial_two,
    owner_rotation,
    owner_axial,
    owner_angle,
    turn_table,
    angular_table,
):
    leaf_size, state_size, sub_size = dims
    group = state_size * sub_size
    holders = leaf_size * group
    degrees, morders = sphere_coef.shape[:2]
    slots = sphere_coef.shape[-1]
    bf16 = jnp.bfloat16
    f32 = jnp.float32

    leaf_code = leaf_octant * 2 + leaf_parent
    member = cluster[:, None] == jnp.arange(leaf_code.shape[0], dtype=jnp.int32)[None, :]
    code = jnp.sum(jnp.where(member, leaf_code[None, :], 0), axis=1)
    alive = jnp.arange(slots, dtype=jnp.int32) // (slots // SBLK) < live_blocks[0]
    code = jnp.where(alive, code, -1)
    code = jnp.broadcast_to(code[None, :], (8, slots)).reshape(8 * slots, 1)

    xs = jnp.transpose(sphere_coef, (0, 2, 1, 3, 4, 5)).reshape(degrees, 2, morders, 8 * slots)
    xs = pad_last(xs, QP, 8 * slots).reshape(degrees * 2 * QP, 8 * slots)
    turns = jnp.transpose(rotation, (1, 2, 0, 3, 4))
    f = rotation_blocks(turns[0], turns[1])
    s1 = axial_rows(jnp.transpose(axial_one, (0, 2, 3, 5, 4, 1)))
    s2 = axial_rows(jnp.transpose(axial_two, (0, 2, 3, 5, 4, 1)))
    rows = degrees * 2 * QP
    vmem = pl.BlockSpec(memory_space=pltpu.VMEM)
    packed = pl.pallas_call(
        functools.partial(local_kernel, morders),
        out_shape=jax.ShapeDtypeStruct((rows // 16, 128), f32),
        in_specs=[pl.BlockSpec(memory_space=pltpu.SMEM)] + [vmem] * 5,
        out_specs=vmem,
        scratch_shapes=[
            pltpu.VMEM((rows, 128), bf16),
            pltpu.VMEM((LP * 2 * QP, 128), f32),
            pltpu.VMEM((LP * 2 * QP, 128), f32),
            pltpu.VMEM((QP * 2 * LP, 128), f32),
            pltpu.VMEM((QP * 2 * LP, 128), f32),
        ],
        compiler_params=pltpu.CompilerParams(vmem_limit_bytes=32 * 1024 * 1024),
    )(box_octant, xs, code, f, s1, s2)

    fo = rotation_blocks(owner_rotation[0, 0], owner_rotation[0, 1])
    nloc = turn_table.shape[1]
    orders = turn_table.shape[3]
    so = axial_rows(jnp.transpose(owner_axial[0], (0, 1, 2, 5, 4, 3)))
    turn = pad_last(turn_table[0], QP, orders)
    own = angular_table.shape[0]
    ang = jnp.transpose(angular_table, (1, 2, 0)).reshape(2, nloc // 2, -1, own)
    ang = jnp.concatenate([ang[0], ang[1]], axis=-1).astype(f32)
    lats = ang.shape[1] // 2
    assert own == 64 and lats == holders and orders == 64 * leaf_size

    out = pl.pallas_call(
        functools.partial(owner_kernel, dims),
        out_shape=jax.ShapeDtypeStruct((16, PHI), f32),
        in_specs=[vmem] * 3 + [pl.BlockSpec(memory_space=pltpu.SMEM)] + [vmem] * 2,
        out_specs=vmem,
        scratch_shapes=[
            pltpu.VMEM((group - 1, rows // 16, 128), f32),
            pltpu.VMEM((morders, 2 * nloc, 64), bf16),
            pltpu.VMEM((LP * 2 * QP, 128), f32),
            pltpu.VMEM((QP * 2 * nloc, 128), f32),
            pltpu.VMEM((nloc, 16, orders), f32),
            pltpu.VMEM((leaf_size, 8 * nloc, 128), bf16),
            pltpu.VMEM((leaf_size - 1, 8 * nloc, 128), bf16),
            pltpu.VMEM((8 * nloc, 128), f32),
            pltpu.VMEM((lats, 16, 128), bf16),
            pltpu.VMEM((holders, 16, 128), bf16),
            pltpu.VMEM((orders, PHI), bf16),
            pltpu.VMEM((orders, PHI), bf16),
            pltpu.SemaphoreType.DMA((group - 1,)),
            pltpu.SemaphoreType.DMA((group - 1,)),
            pltpu.SemaphoreType.DMA((leaf_size - 1,)),
            pltpu.SemaphoreType.DMA((leaf_size - 1,)),
            pltpu.SemaphoreType.DMA((holders - 1,)),
            pltpu.SemaphoreType.DMA((holders - 1,)),
        ],
        compiler_params=pltpu.CompilerParams(
            collective_id=0, has_side_effects=True, vmem_limit_bytes=48 * 1024 * 1024
        ),
    )(packed, fo, so, owner_angle, turn, ang)
    out = out.reshape(2, 2, 4, PHI)
    return jnp.transpose(out, (2, 0, 1, 3))[None]


def solution(mesh):
    dims = (mesh.shape["leaf"], mesh.shape["state"], mesh.shape["sub"])
    split = ("groups", "leaf", "state", "sub")
    return jax.shard_map(
        functools.partial(on_device, dims),
        mesh=mesh,
        in_specs=(
            P(None, None, None, None, None, split),
            P(split),
            P(split),
            P(split),
            P(split),
            P(split),
            P(),
            P(),
            P(),
            P(("groups", "leaf"), None, None, None, None),
            P(("groups", "leaf"), None, None, None, ("state", "sub"), None, None),
            P("groups"),
            P(("groups", "leaf"), ("state", "sub"), None, None),
            P("leaf", ("state", "sub"), None),
        ),
        out_specs=P(split, None, None, None, None),
        check_vma=False,
    )
```

```python
import functools
import math

import jax
import jax.numpy as jnp
from jax import lax
from jax.experimental import pallas as pl
from jax.experimental.pallas import tpu as pltpu
from jax.sharding import PartitionSpec as P

SBLK = 4
PHI = 2048
LP = 16
QP = 32
MESH = pl.DeviceIdType.MESH


def lane_ids():
    lane = lax.broadcasted_iota(jnp.int32, (1, 128), 1)
    return lane, (lane % 64) // 4


def spread_matrix():
    row = lax.broadcasted_iota(jnp.int32, (128, 128), 0)
    col = lax.broadcasted_iota(jnp.int32, (128, 128), 1)
    same = (row // 64 == col // 64) & (row % 4 == col % 4)
    return jnp.where(same, 1.0, 0.0).astype(jnp.bfloat16)


def dot(a, b):
    return jnp.dot(a, b, preferred_element_type=jnp.float32)


def axial_operand(y_ref, q):
    lane, _ = lane_ids()
    low = lane < 64
    real, imag = [y_ref[pl.ds(part * QP + q, LP, stride=2 * QP), :] for part in range(2)]
    real_turned = pltpu.roll(real, 64, 1)
    imag_turned = pltpu.roll(imag, 64, 1)
    return jnp.concatenate(
        [
            jnp.where(low, real, imag_turned),
            jnp.where(low, real_turned, imag),
            jnp.where(low, -imag, real_turned),
            jnp.where(low, -imag_turned, real),
        ],
        axis=0,
    ).astype(jnp.bfloat16)


def axial_result(r):
    lane, _ = lane_ids()
    low = lane < 64
    half = r.shape[0] // 2
    first, second = r[:half], r[half:]
    real = jnp.where(low, first, pltpu.roll(second, 64, 1))
    imag = jnp.where(low, pltpu.roll(first, 64, 1), second)
    return real, imag


def identity(rows):
    row = lax.broadcasted_iota(jnp.int32, (rows, 128), 0)
    col = lax.broadcasted_iota(jnp.int32, (rows, 128), 1)
    return jnp.where(row == col, 1.0, 0.0).astype(jnp.bfloat16)


def dot_nt(a, b):
    return lax.dot_general(a, b, (((1,), (1,)), ((), ())), preferred_element_type=jnp.float32)


def axial_matrices(s_ref, a_ref, degrees):
    eye = identity(QP)
    zeros = jnp.zeros((64, 128), jnp.float32)
    for u in range(2):
        for w in range(degrees):
            pieces = []
            for part in range(2):
                base = ((part * 2 + u) * degrees + w) * degrees * 2
                for t in range(2):
                    pieces.append(s_ref[pl.ds(base + t, LP, stride=2), :])
            block = jnp.concatenate(pieces + [zeros], axis=0).astype(jnp.bfloat16)
            a_ref[pl.ds(u * LP + w, QP, stride=2 * LP), :] = dot_nt(eye, block)


def rotation_matrices(w_ref, f_ref, orders):
    degrees = f_ref.shape[0]

    def body(l, carry):
        for o in range(8):
            base = (o * degrees + l) * orders * 2
            real = w_ref[pl.ds(base, QP, stride=2), :]
            imag = w_ref[pl.ds(base + 1, QP, stride=2), :]
            f_ref[l, o, :QP, :] = (real - pltpu.roll(imag, QP, 1)).astype(jnp.bfloat16)
            f_ref[l, o, QP:, :] = (imag + pltpu.roll(real, QP, 1)).astype(jnp.bfloat16)
        return carry

    lax.fori_loop(0, degrees, body, 0)


def axial_pass(y_ref, z_ref, a_ref, orders):
    for q in range(orders):
        mats = a_ref[q * 2 * LP : (q + 1) * 2 * LP, :][:, :64].astype(jnp.bfloat16)
        for part, z in enumerate(axial_result(dot(mats, axial_operand(y_ref, q)))):
            z_ref[pl.ds(part * QP + q, LP, stride=2 * QP), :] = z


def local_kernel(
    orders,
    box_ref,
    live_ref,
    octant_ref,
    parent_ref,
    xs_ref,
    cluster_ref,
    w_ref,
    s1_ref,
    s2_ref,
    out_ref,
    v_ref,
    y_ref,
    z_ref,
    a1_ref,
    a2_ref,
    f_ref,
):
    degrees = f_ref.shape[0]
    for s_ref, a_ref in ((s1_ref, a1_ref), (s2_ref, a2_ref)):
        a_ref[...] = jnp.zeros_like(a_ref)
        axial_matrices(s_ref, a_ref, degrees)
    lane, rep = lane_ids()
    width = 2 * QP
    y_ref[...] = jnp.zeros_like(y_ref)
    z_ref[...] = jnp.zeros_like(z_ref)
    rotation_matrices(w_ref, f_ref, orders)
    slots = xs_ref.shape[1] // 8
    cluster = cluster_ref[...]
    code = jnp.full((1, slots), -1, jnp.int32)
    for leaf in range(octant_ref.shape[0]):
        code = jnp.where(cluster == leaf, octant_ref[leaf] * 2 + parent_ref[leaf], code)
    slot = lax.broadcasted_iota(jnp.int32, (1, slots), 1)
    code = jnp.where(slot // (slots // SBLK) < live_ref[0], code, -1)
    code = jnp.concatenate([code] * 8, axis=1)
    row = lax.broadcasted_iota(jnp.int32, (128, 8 * slots), 0)
    col = lax.broadcasted_iota(jnp.int32, (128, 8 * slots), 1) // slots
    keep = (row // 64 == col // 4) & (row % 4 == col % 4) & ((row % 64) // 4 == code)
    spread = jnp.where(keep, 1.0, 0.0).astype(jnp.bfloat16)
    v_ref[...] = dot_nt(xs_ref[...], spread).astype(jnp.bfloat16)
    octant = rep // 2
    box = rep % 2

    for level in range(2):
        for l in range(degrees):
            v = v_ref[l * width : (l + 1) * width, :]
            if level == 0:
                r = dot(f_ref[l].reshape(8 * width, 128)[:, :width], v)
                acc = r[:width]
                for o in range(1, 8):
                    acc = jnp.where(octant == o, r[o * width : (o + 1) * width], acc)
            else:
                acc = dot(f_ref[l, box_ref[0]][:, :width], v)
                acc = jnp.where(box == 1, dot(f_ref[l, box_ref[1]][:, :width], v), acc)
            y_ref[l * width : (l + 1) * width, :] = acc
        axial_pass(y_ref, z_ref, a1_ref if level == 0 else a2_ref, orders)
        for l in range(degrees):
            z = z_ref[l * width : (l + 1) * width, :]
            if level == 0:
                mats = f_ref[l].reshape(8 * width, 128)[:, :width]
                parts = [jnp.where(octant == o, z, 0.0) for o in range(8)]
            else:
                mats = jnp.concatenate([f_ref[l, box_ref[b]][:, :width] for b in range(2)], axis=0)
                parts = [jnp.where(box == b, z, 0.0) for b in range(2)]
            stacked = jnp.concatenate(parts, axis=0).astype(jnp.bfloat16)
            r = lax.dot_general(
                mats, stacked, (((0,), (0,)), ((), ())), preferred_element_type=jnp.float32
            )
            if level == 0:
                v_ref[l * width : (l + 1) * width, :] = r.astype(jnp.bfloat16)
            else:
                y_ref[l * width : (l + 1) * width, :] = r
    total = degrees * width
    m = y_ref[:total, :]
    hi = m.astype(jnp.bfloat16)
    lo = (m - hi.astype(jnp.float32)).astype(jnp.bfloat16)
    mix = spread_matrix()
    full = dot(hi, mix) + dot(lo, mix)
    rows = total // 16
    packed = full[:rows]
    for r in range(1, 16):
        packed = jnp.where(rep == r, full[r * rows : (r + 1) * rows], packed)
    out_ref[...] = packed


def circle(steps):
    steps = jnp.bitwise_and(steps + PHI // 2, PHI - 1) - PHI // 2
    x = steps.astype(jnp.float32) * (0.5 * math.pi / PHI)
    x2 = x * x
    sine = x * (1 + x2 * (-1 / 6 + x2 * (1 / 120 + x2 * (-1 / 5040 + x2 * (1 / 362880)))))
    cosine = 1 + x2 * (-1 / 2 + x2 * (1 / 24 + x2 * (-1 / 720 + x2 * (1 / 40320))))
    for _ in range(2):
        sine, cosine = 2 * sine * cosine, 1 - 2 * sine * sine
    return cosine, sine


def make_tables(tab_c, tab_s):
    orders = tab_c.shape[0]
    j = lax.broadcasted_iota(jnp.int32, (16, 128), 0) - orders // 2
    k = lax.broadcasted_iota(jnp.int32, (16, 128), 1)
    turns = []
    for a in range(PHI // 128):
        turns.append(circle(j * (128 * a)))

    def body(i, carry):
        r0 = pl.multiple_of(i * 16, 16)
        c1, s1 = circle((j + r0) * k)
        for a, (c2, s2) in enumerate(turns):
            cols = slice(a * 128, (a + 1) * 128)
            tab_c[pl.ds(r0, 16), cols] = (c1 * c2 - s1 * s2).astype(jnp.bfloat16)
            tab_s[pl.ds(r0, 16), cols] = (s1 * c2 + c1 * s2).astype(jnp.bfloat16)
        return carry

    lax.fori_loop(0, orders // 16, body, 0)


def owner_kernel(
    dims,
    packed_ref,
    fo_ref,
    so_ref,
    angle_ref,
    turn_ref,
    ang_ref,
    out_ref,
    recv1,
    ao_ref,
    y_ref,
    zq_ref,
    vals_ref,
    sbuf,
    recv2,
    root_ref,
    fbuf,
    recv3,
    tab_c,
    tab_s,
    send1,
    rsem1,
    send2,
    rsem2,
    send3,
    rsem3,
):
    leaf_size, state_size, sub_size = dims
    group = state_size * sub_size
    holders = leaf_size * group
    my_groups = lax.axis_index("groups")
    my_leaf = lax.axis_index("leaf")
    my_state = lax.axis_index("state")
    my_sub = lax.axis_index("sub")
    my_g = my_state * sub_size + my_sub
    me = my_leaf * group + my_g
    degrees = fo_ref.shape[0]
    q_orders = ao_ref.shape[0]
    nloc = turn_ref.shape[0]
    orders = turn_ref.shape[2]
    width = 2 * QP
    lane, rep = lane_ids()
    low = lane < 64

    def device(index):
        g = lax.rem(index, group)
        return (my_groups, index // group, g // sub_size, lax.rem(g, sub_size))

    barrier = pltpu.get_barrier_semaphore()

    def greet(d, carry):
        pl.semaphore_signal(
            barrier, inc=1, device_id=device(lax.rem(me + d, holders)), device_id_type=MESH
        )
        return carry

    lax.fori_loop(1, holders, greet, 0)
    pl.semaphore_wait(barrier, holders - 1)

    copies = []
    for d in range(1, group):
        target = my_leaf * group + lax.rem(my_g + d, group)
        copy = pltpu.make_async_remote_copy(
            src_ref=packed_ref,
            dst_ref=recv1.at[d - 1],
            send_sem=send1.at[d - 1],
            recv_sem=rsem1.at[d - 1],
            device_id=device(target),
            device_id_type=MESH,
        )
        copy.start()
        copies.append(copy)

    y_ref[...] = jnp.zeros_like(y_ref)
    zq_ref[...] = jnp.zeros_like(zq_ref)
    eye = identity(2 * nloc)
    for q in range(q_orders):
        pieces = []
        for part in range(2):
            for t in range(2):
                first, second = [
                    so_ref[
                        pl.ds(((part * q_orders + q) * 2 + u) * degrees * 2 + t, LP, stride=2), :
                    ]
                    for u in range(2)
                ]
                pieces.append(first + pltpu.roll(second, nloc, 1))
        ao_ref[q] = dot_nt(eye, jnp.concatenate(pieces, axis=0).astype(jnp.bfloat16)).astype(
            jnp.bfloat16
        )
    azimuth = angle_ref[my_leaf]
    order_values = (
        lax.broadcasted_iota(jnp.int32, (8, orders), 1) - orders // 2
    ).astype(jnp.float32)
    cosine = jnp.cos(order_values * azimuth)
    sine = jnp.sin(order_values * azimuth)
    sine = jnp.where(lax.broadcasted_iota(jnp.int32, (8, orders), 0) < 4, sine, -sine)

    for copy in copies:
        copy.wait()
    packed = packed_ref[...]
    for d in range(1, group):
        packed = packed + recv1[d - 1]
    parts = [jnp.where(rep == r, packed, 0.0) for r in range(16)]
    vectors = dot(
        jnp.concatenate(parts, axis=0).astype(jnp.bfloat16), spread_matrix()
    ).astype(jnp.bfloat16)
    for l in range(degrees):
        y_ref[l * width : (l + 1) * width, :] = dot(
            fo_ref[l], vectors[l * width : (l + 1) * width]
        )
    for q in range(q_orders):
        for part, z in enumerate(axial_result(dot(ao_ref[q], axial_operand(y_ref, q)))):
            start = (q * 2 + part) * nloc
            zq_ref[start : start + nloc, :] = z

    for block in range(nloc // 8):
        gathered = jnp.zeros((QP, 128), jnp.float32)
        for n8 in range(8):
            n = block * 8 + n8
            real = zq_ref[pl.ds(n, QP, stride=2 * nloc), :]
            imag = zq_ref[pl.ds(nloc + n, QP, stride=2 * nloc), :]
            both = jnp.where(rep % 2 == 0, real, imag)
            gathered = jnp.where(rep // 2 == n8, both, gathered)
        flipped = gathered.T
        for n8 in range(8):
            n = block * 8 + n8
            framed = jnp.concatenate(
                [flipped[n8 * 8 : n8 * 8 + 8], flipped[64 + n8 * 8 : 72 + n8 * 8]], axis=0
            ).astype(jnp.bfloat16)
            values = dot(framed, turn_ref[n])
            for u in range(2):
                v = values[u * 8 : u * 8 + 8]
                vals_ref[n, u * 8 : u * 8 + 8, :] = cosine * v + sine * pltpu.roll(v, 4, 0)

    half = nloc // 2
    for m in range(orders // 128):
        cols = slice(m * 128, (m + 1) * 128)
        for n in range(half):
            a = vals_ref[n, :, cols]
            b = vals_ref[n + half, :, cols]
            rows = slice(n * 16, (n + 1) * 16)
            sbuf[2 * m, rows, :] = jnp.where(low, a, pltpu.roll(b, 64, 1)).astype(jnp.bfloat16)
            sbuf[2 * m + 1, rows, :] = jnp.where(low, pltpu.roll(a, 64, 1), b).astype(
                jnp.bfloat16
            )

    copies = []
    for d in range(1, leaf_size):
        to_leaf = lax.rem(my_leaf + d, leaf_size)
        copy = pltpu.make_async_remote_copy(
            src_ref=sbuf.at[to_leaf],
            dst_ref=recv2.at[d - 1],
            send_sem=send2.at[d - 1],
            recv_sem=rsem2.at[d - 1],
            device_id=device(to_leaf * group + my_g),
            device_id_type=MESH,
        )
        copy.start()
        copies.append(copy)
    make_tables(tab_c, tab_s)
    for copy in copies:
        copy.wait()
    root = sbuf[my_leaf].astype(jnp.float32)
    for d in range(1, leaf_size):
        root = root + recv2[d - 1].astype(jnp.float32)
    root_ref[...] = root.astype(jnp.bfloat16).astype(jnp.float32)

    lats = ang_ref.shape[1] // 2
    sign = jnp.where(lax.broadcasted_iota(jnp.int32, (8, 128), 0) < 4, -1.0, 1.0)

    def field_copy(d):
        target = lax.rem(me + d, holders)
        return pltpu.make_async_remote_copy(
            src_ref=fbuf.at[target],
            dst_ref=recv3.at[me],
            send_sem=send3.at[d - 1],
            recv_sem=rsem3.at[d - 1],
            device_id=device(target),
            device_id_type=MESH,
        )

    def latitude(h):
        theta = jnp.zeros((8, 128), jnp.float32)
        cross = jnp.zeros((8, 128), jnp.float32)
        for n in range(half):
            a0 = ang_ref[n, pl.ds(h, 1), :]
            a1 = ang_ref[n, pl.ds(lats + h, 1), :]
            r0 = root_ref[n * 16 : n * 16 + 8, :]
            r1 = root_ref[n * 16 + 8 : n * 16 + 16, :]
            theta = theta + (a0 * r0 + a1 * r1)
            cross = cross + (a1 * r0 + a0 * r1)
        theta = theta + pltpu.roll(theta, 64, 1)
        cross = cross + pltpu.roll(cross, 64, 1)
        phi = sign * pltpu.roll(cross, 4, 0)
        fbuf[h] = jnp.concatenate([theta, phi], axis=0).astype(jnp.bfloat16)

    def start(d, carry):
        latitude(lax.rem(me + d, holders))
        field_copy(d).start()
        return carry

    def finish(d, carry):
        field_copy(d).wait_send()
        source = lax.rem(me + holders - d, holders)
        pltpu.make_async_remote_copy(
            src_ref=fbuf.at[source],
            dst_ref=recv3.at[source],
            send_sem=send3.at[d - 1],
            recv_sem=rsem3.at[d - 1],
            device_id=device(source),
            device_id_type=MESH,
        ).wait_recv()
        return carry

    lax.fori_loop(1, holders, start, 0)
    latitude(me)
    recv3[me] = fbuf[me]
    lax.fori_loop(1, holders, finish, 0)

    pieces = []
    for leaf in range(leaf_size):
        total = recv3[leaf * group].astype(jnp.float32)
        for g in range(1, group):
            total = total + recv3[leaf * group + g].astype(jnp.float32)
        pieces.append(total)
    spectrum = jnp.concatenate(
        [
            jnp.where(low, pieces[2 * m], pieces[2 * m + 1]).astype(jnp.bfloat16)
            for m in range(leaf_size // 2)
        ],
        axis=1,
    )
    scale = 1.0 / math.sqrt(orders)
    for tile in range(PHI // 512):
        cols = slice(tile * 512, (tile + 1) * 512)
        first = dot(spectrum, tab_c[:, cols])
        second = dot(spectrum, tab_s[:, cols])
        for c in range(2):
            rows = slice(c * 8, c * 8 + 8)
            turned = pltpu.roll(second[rows], 4, 0)
            out_ref[rows, cols] = (first[rows] + jnp.tile(sign, (1, 4)) * turned) * scale


def pad_last(x, *sizes):
    skip = x.ndim - len(sizes)
    return jnp.pad(
        x, [(0, 0)] * skip + [(0, s - n) for s, n in zip(sizes, x.shape[skip:], strict=True)]
    )


def rotation_blocks(real, imag):
    real = pad_last(real.astype(jnp.bfloat16), QP, QP)
    imag = pad_last(imag.astype(jnp.bfloat16), QP, QP)
    return jnp.concatenate(
        [jnp.concatenate([real, -imag], -1), jnp.concatenate([imag, real], -1)], -2
    )


def axial_rows(mats):
    mats = mats.reshape(-1, mats.shape[-1])
    return jnp.pad(mats, ((0, 16), (0, 128 - mats.shape[1])))


def on_device(
    dims,
    sphere_coef,
    live_blocks,
    cluster,
    leaf_parent,
    leaf_octant,
    box_octant,
    rotation,
    axial_one,
    axial_two,
    owner_rotation,
    owner_axial,
    owner_angle,
    turn_table,
    angular_table,
):
    leaf_size, state_size, sub_size = dims
    group = state_size * sub_size
    holders = leaf_size * group
    degrees, morders = sphere_coef.shape[:2]
    slots = sphere_coef.shape[-1]
    bf16 = jnp.bfloat16
    f32 = jnp.float32

    xs = jnp.transpose(sphere_coef, (0, 2, 1, 3, 4, 5)).reshape(degrees, 2, morders, 8 * slots)
    xs = pad_last(xs, QP, 8 * slots).reshape(degrees * 2 * QP, 8 * slots)
    w = jnp.transpose(rotation, (0, 2, 3, 1, 4)).reshape(-1, morders)
    w = jnp.pad(w, ((0, 16), (0, 128 - morders)))
    s1 = axial_rows(jnp.transpose(axial_one, (0, 2, 3, 5, 4, 1)))
    s2 = axial_rows(jnp.transpose(axial_two, (0, 2, 3, 5, 4, 1)))
    rows = degrees * 2 * QP
    vmem = pl.BlockSpec(memory_space=pltpu.VMEM)
    packed = pl.pallas_call(
        functools.partial(local_kernel, morders),
        out_shape=jax.ShapeDtypeStruct((rows // 16, 128), f32),
        in_specs=[pl.BlockSpec(memory_space=pltpu.SMEM)] * 4 + [vmem] * 5,
        out_specs=vmem,
        scratch_shapes=[
            pltpu.VMEM((rows, 128), bf16),
            pltpu.VMEM((LP * 2 * QP, 128), f32),
            pltpu.VMEM((LP * 2 * QP, 128), f32),
            pltpu.VMEM((QP * 2 * LP, 128), f32),
            pltpu.VMEM((QP * 2 * LP, 128), f32),
            pltpu.VMEM((degrees, 8, 2 * QP, 128), bf16),
        ],
        compiler_params=pltpu.CompilerParams(vmem_limit_bytes=32 * 1024 * 1024),
    )(
        box_octant,
        live_blocks,
        leaf_octant,
        leaf_parent,
        xs,
        cluster.reshape(1, slots),
        w,
        s1,
        s2,
    )

    fo = rotation_blocks(owner_rotation[0, 0], owner_rotation[0, 1])
    nloc = turn_table.shape[1]
    orders = turn_table.shape[3]
    so = axial_rows(jnp.transpose(owner_axial[0], (0, 1, 2, 5, 4, 3)))
    turn = pad_last(turn_table[0], QP, orders)
    own = angular_table.shape[0]
    ang = jnp.transpose(angular_table, (1, 2, 0)).reshape(2, nloc // 2, -1, own)
    ang = jnp.concatenate([ang[0], ang[1]], axis=-1).astype(f32)
    lats = ang.shape[1] // 2
    assert own == 64 and lats == holders and orders == 64 * leaf_size

    out = pl.pallas_call(
        functools.partial(owner_kernel, dims),
        out_shape=jax.ShapeDtypeStruct((16, PHI), f32),
        in_specs=[vmem] * 3 + [pl.BlockSpec(memory_space=pltpu.SMEM)] + [vmem] * 2,
        out_specs=vmem,
        scratch_shapes=[
            pltpu.VMEM((group - 1, rows // 16, 128), f32),
            pltpu.VMEM((morders, 2 * nloc, 64), bf16),
            pltpu.VMEM((LP * 2 * QP, 128), f32),
            pltpu.VMEM((QP * 2 * nloc, 128), f32),
            pltpu.VMEM((nloc, 16, orders), f32),
            pltpu.VMEM((leaf_size, 8 * nloc, 128), bf16),
            pltpu.VMEM((leaf_size - 1, 8 * nloc, 128), bf16),
            pltpu.VMEM((8 * nloc, 128), f32),
            pltpu.VMEM((lats, 16, 128), bf16),
            pltpu.VMEM((holders, 16, 128), bf16),
            pltpu.VMEM((orders, PHI), bf16),
            pltpu.VMEM((orders, PHI), bf16),
            pltpu.SemaphoreType.DMA((group - 1,)),
            pltpu.SemaphoreType.DMA((group - 1,)),
            pltpu.SemaphoreType.DMA((leaf_size - 1,)),
            pltpu.SemaphoreType.DMA((leaf_size - 1,)),
            pltpu.SemaphoreType.DMA((holders - 1,)),
            pltpu.SemaphoreType.DMA((holders - 1,)),
        ],
        compiler_params=pltpu.CompilerParams(
            collective_id=0, has_side_effects=True, vmem_limit_bytes=48 * 1024 * 1024
        ),
    )(packed, fo, so, owner_angle, turn, ang)
    out = out.reshape(2, 2, 4, PHI)
    return jnp.transpose(out, (2, 0, 1, 3))[None]


def solution(mesh):
    dims = (mesh.shape["leaf"], mesh.shape["state"], mesh.shape["sub"])
    split = ("groups", "leaf", "state", "sub")
    return jax.shard_map(
        functools.partial(on_device, dims),
        mesh=mesh,
        in_specs=(
            P(None, None, None, None, None, split),
            P(split),
            P(split),
            P(split),
            P(split),
            P(split),
            P(),
            P(),
            P(),
            P(("groups", "leaf"), None, None, None, None),
            P(("groups", "leaf"), None, None, None, ("state", "sub"), None, None),
            P("groups"),
            P(("groups", "leaf"), ("state", "sub"), None, None),
            P("leaf", ("state", "sub"), None),
        ),
        out_specs=P(split, None, None, None, None),
        check_vma=False,
    )
```

```python
import functools
import math

import jax
import jax.numpy as jnp
from jax import lax
from jax.experimental import pallas as pl
from jax.experimental.pallas import tpu as pltpu
from jax.sharding import PartitionSpec as P

SBLK = 4
PHI = 2048
LP = 16
QP = 32
MESH = pl.DeviceIdType.MESH


def lane_ids():
    lane = lax.broadcasted_iota(jnp.int32, (1, 128), 1)
    return lane, (lane % 64) // 4


def spread_matrix():
    row = lax.broadcasted_iota(jnp.int32, (128, 128), 0)
    col = lax.broadcasted_iota(jnp.int32, (128, 128), 1)
    same = (row // 64 == col // 64) & (row % 4 == col % 4)
    return jnp.where(same, 1.0, 0.0).astype(jnp.bfloat16)


def dot(a, b):
    return jnp.dot(a, b, preferred_element_type=jnp.float32)


def axial_operand(y_ref, q):
    lane, _ = lane_ids()
    low = lane < 64
    real, imag = [y_ref[pl.ds(part * QP + q, LP, stride=2 * QP), :] for part in range(2)]
    real_turned = pltpu.roll(real, 64, 1)
    imag_turned = pltpu.roll(imag, 64, 1)
    return jnp.concatenate(
        [
            jnp.where(low, real, imag_turned),
            jnp.where(low, real_turned, imag),
            jnp.where(low, -imag, real_turned),
            jnp.where(low, -imag_turned, real),
        ],
        axis=0,
    ).astype(jnp.bfloat16)


def axial_result(r):
    lane, _ = lane_ids()
    low = lane < 64
    half = r.shape[0] // 2
    first, second = r[:half], r[half:]
    real = jnp.where(low, first, pltpu.roll(second, 64, 1))
    imag = jnp.where(low, pltpu.roll(first, 64, 1), second)
    return real, imag


def identity(rows):
    row = lax.broadcasted_iota(jnp.int32, (rows, 128), 0)
    col = lax.broadcasted_iota(jnp.int32, (rows, 128), 1)
    return jnp.where(row == col, 1.0, 0.0).astype(jnp.bfloat16)


def dot_nt(a, b):
    return lax.dot_general(a, b, (((1,), (1,)), ((), ())), preferred_element_type=jnp.float32)


def axial_matrices(s_ref, a_ref, degrees):
    eye = identity(QP)
    zeros = jnp.zeros((64, 128), jnp.float32)
    for u in range(2):
        for w in range(degrees):
            pieces = []
            for part in range(2):
                base = ((part * 2 + u) * degrees + w) * degrees * 2
                for t in range(2):
                    pieces.append(s_ref[pl.ds(base + t, LP, stride=2), :])
            block = jnp.concatenate(pieces + [zeros], axis=0).astype(jnp.bfloat16)
            a_ref[pl.ds(u * LP + w, QP, stride=2 * LP), :] = dot_nt(eye, block)


def rotation_matrices(w_ref, f_ref, orders):
    degrees = f_ref.shape[0]

    def body(l, carry):
        for o in range(8):
            base = (o * degrees + l) * orders * 2
            real = w_ref[pl.ds(base, QP, stride=2), :]
            imag = w_ref[pl.ds(base + 1, QP, stride=2), :]
            f_ref[l, o, :QP, :] = (real - pltpu.roll(imag, QP, 1)).astype(jnp.bfloat16)
            f_ref[l, o, QP:, :] = (imag + pltpu.roll(real, QP, 1)).astype(jnp.bfloat16)
        return carry

    lax.fori_loop(0, degrees, body, 0)


def axial_pass(y_ref, z_ref, a_ref, orders):
    for q in range(orders):
        mats = a_ref[q * 2 * LP : (q + 1) * 2 * LP, :][:, :64].astype(jnp.bfloat16)
        for part, z in enumerate(axial_result(dot(mats, axial_operand(y_ref, q)))):
            z_ref[pl.ds(part * QP + q, LP, stride=2 * QP), :] = z


def local_kernel(
    orders,
    box_ref,
    live_ref,
    octant_ref,
    parent_ref,
    xs_ref,
    cluster_ref,
    w_ref,
    s1_ref,
    s2_ref,
    out_ref,
    v_ref,
    y_ref,
    z_ref,
    a1_ref,
    a2_ref,
    f_ref,
):
    degrees = f_ref.shape[0]
    for s_ref, a_ref in ((s1_ref, a1_ref), (s2_ref, a2_ref)):
        a_ref[...] = jnp.zeros_like(a_ref)
        axial_matrices(s_ref, a_ref, degrees)
    lane, rep = lane_ids()
    width = 2 * QP
    y_ref[...] = jnp.zeros_like(y_ref)
    z_ref[...] = jnp.zeros_like(z_ref)
    rotation_matrices(w_ref, f_ref, orders)
    slots = xs_ref.shape[1]
    cluster = cluster_ref[...]
    code = jnp.full((1, slots), -1, jnp.int32)
    for leaf in range(octant_ref.shape[0]):
        code = jnp.where(cluster == leaf, octant_ref[leaf] * 2 + parent_ref[leaf], code)
    slot = lax.broadcasted_iota(jnp.int32, (1, slots), 1)
    code = jnp.where(slot // (slots // SBLK) < live_ref[0], code, -1)
    place = lax.broadcasted_iota(jnp.int32, (128, slots), 0)
    spread = jnp.where((place % 64) // 4 == code, 1.0, 0.0).astype(jnp.bfloat16)
    count = 16 * orders
    kind = lax.broadcasted_iota(jnp.int32, (count, 128), 0) % 8
    keep = (kind // 4 == lane // 64) & (kind % 4 == lane % 4)
    row = lax.broadcasted_iota(jnp.int32, (width, count), 0)
    col = lax.broadcasted_iota(jnp.int32, (width, count), 1)
    pick = jnp.where((col // 16 == row % QP) & ((col // 8) % 2 == row // QP), 1.0, 0.0)
    pick = pick.astype(jnp.bfloat16)
    for l in range(degrees):
        r = dot_nt(xs_ref[l * count : (l + 1) * count, :], spread)
        r = jnp.where(keep, r, 0.0).astype(jnp.bfloat16)
        v_ref[l * width : (l + 1) * width, :] = dot(pick, r).astype(jnp.bfloat16)
    octant = rep // 2
    box = rep % 2

    for level in range(2):
        for l in range(degrees):
            v = v_ref[l * width : (l + 1) * width, :]
            if level == 0:
                r = dot(f_ref[l].reshape(8 * width, 128)[:, :width], v)
                acc = r[:width]
                for o in range(1, 8):
                    acc = jnp.where(octant == o, r[o * width : (o + 1) * width], acc)
            else:
                acc = dot(f_ref[l, box_ref[0]][:, :width], v)
                acc = jnp.where(box == 1, dot(f_ref[l, box_ref[1]][:, :width], v), acc)
            y_ref[l * width : (l + 1) * width, :] = acc
        axial_pass(y_ref, z_ref, a1_ref if level == 0 else a2_ref, orders)
        for l in range(degrees):
            z = z_ref[l * width : (l + 1) * width, :]
            if level == 0:
                mats = f_ref[l].reshape(8 * width, 128)[:, :width]
                parts = [jnp.where(octant == o, z, 0.0) for o in range(8)]
            else:
                mats = jnp.concatenate([f_ref[l, box_ref[b]][:, :width] for b in range(2)], axis=0)
                parts = [jnp.where(box == b, z, 0.0) for b in range(2)]
            stacked = jnp.concatenate(parts, axis=0).astype(jnp.bfloat16)
            r = lax.dot_general(
                mats, stacked, (((0,), (0,)), ((), ())), preferred_element_type=jnp.float32
            )
            if level == 0:
                v_ref[l * width : (l + 1) * width, :] = r.astype(jnp.bfloat16)
            else:
                y_ref[l * width : (l + 1) * width, :] = r
    total = degrees * width
    m = y_ref[:total, :]
    hi = m.astype(jnp.bfloat16)
    lo = (m - hi.astype(jnp.float32)).astype(jnp.bfloat16)
    mix = spread_matrix()
    full = dot(hi, mix) + dot(lo, mix)
    rows = total // 16
    packed = full[:rows]
    for r in range(1, 16):
        packed = jnp.where(rep == r, full[r * rows : (r + 1) * rows], packed)
    out_ref[...] = packed


def circle(steps):
    steps = jnp.bitwise_and(steps + PHI // 2, PHI - 1) - PHI // 2
    x = steps.astype(jnp.float32) * (0.5 * math.pi / PHI)
    x2 = x * x
    sine = x * (1 + x2 * (-1 / 6 + x2 * (1 / 120 + x2 * (-1 / 5040 + x2 * (1 / 362880)))))
    cosine = 1 + x2 * (-1 / 2 + x2 * (1 / 24 + x2 * (-1 / 720 + x2 * (1 / 40320))))
    for _ in range(2):
        sine, cosine = 2 * sine * cosine, 1 - 2 * sine * sine
    return cosine, sine


def make_tables(tab_c, tab_s):
    orders = tab_c.shape[0]
    j = lax.broadcasted_iota(jnp.int32, (16, 128), 0) - orders // 2
    k = lax.broadcasted_iota(jnp.int32, (16, 128), 1)
    turns = []
    for a in range(PHI // 128):
        turns.append(circle(j * (128 * a)))

    def body(i, carry):
        r0 = pl.multiple_of(i * 16, 16)
        c1, s1 = circle((j + r0) * k)
        for a, (c2, s2) in enumerate(turns):
            cols = slice(a * 128, (a + 1) * 128)
            tab_c[pl.ds(r0, 16), cols] = (c1 * c2 - s1 * s2).astype(jnp.bfloat16)
            tab_s[pl.ds(r0, 16), cols] = (s1 * c2 + c1 * s2).astype(jnp.bfloat16)
        return carry

    lax.fori_loop(0, orders // 16, body, 0)


def owner_kernel(
    dims,
    packed_ref,
    fo_ref,
    so_ref,
    angle_ref,
    turn_ref,
    ang_ref,
    out_ref,
    recv1,
    ao_ref,
    y_ref,
    zq_ref,
    vals_ref,
    sbuf,
    recv2,
    root_ref,
    fbuf,
    recv3,
    tab_c,
    tab_s,
    send1,
    rsem1,
    send2,
    rsem2,
    send3,
    rsem3,
):
    leaf_size, state_size, sub_size = dims
    group = state_size * sub_size
    holders = leaf_size * group
    my_groups = lax.axis_index("groups")
    my_leaf = lax.axis_index("leaf")
    my_state = lax.axis_index("state")
    my_sub = lax.axis_index("sub")
    my_g = my_state * sub_size + my_sub
    me = my_leaf * group + my_g
    degrees = fo_ref.shape[0]
    q_orders = ao_ref.shape[0]
    nloc = turn_ref.shape[0]
    orders = turn_ref.shape[2]
    width = 2 * QP
    lane, rep = lane_ids()
    low = lane < 64

    def device(index):
        g = lax.rem(index, group)
        return (my_groups, index // group, g // sub_size, lax.rem(g, sub_size))

    barrier = pltpu.get_barrier_semaphore()

    def greet(d, carry):
        pl.semaphore_signal(
            barrier, inc=1, device_id=device(lax.rem(me + d, holders)), device_id_type=MESH
        )
        return carry

    lax.fori_loop(1, holders, greet, 0)
    pl.semaphore_wait(barrier, holders - 1)

    copies = []
    for d in range(1, group):
        target = my_leaf * group + lax.rem(my_g + d, group)
        copy = pltpu.make_async_remote_copy(
            src_ref=packed_ref,
            dst_ref=recv1.at[d - 1],
            send_sem=send1.at[d - 1],
            recv_sem=rsem1.at[d - 1],
            device_id=device(target),
            device_id_type=MESH,
        )
        copy.start()
        copies.append(copy)

    y_ref[...] = jnp.zeros_like(y_ref)
    zq_ref[...] = jnp.zeros_like(zq_ref)
    eye = identity(2 * nloc)
    for q in range(q_orders):
        pieces = []
        for part in range(2):
            for t in range(2):
                first, second = [
                    so_ref[
                        pl.ds(((part * q_orders + q) * 2 + u) * degrees * 2 + t, LP, stride=2), :
                    ]
                    for u in range(2)
                ]
                pieces.append(first + pltpu.roll(second, nloc, 1))
        ao_ref[q] = dot_nt(eye, jnp.concatenate(pieces, axis=0).astype(jnp.bfloat16)).astype(
            jnp.bfloat16
        )
    azimuth = angle_ref[my_leaf]
    order_values = (
        lax.broadcasted_iota(jnp.int32, (8, orders), 1) - orders // 2
    ).astype(jnp.float32)
    cosine = jnp.cos(order_values * azimuth)
    sine = jnp.sin(order_values * azimuth)
    sine = jnp.where(lax.broadcasted_iota(jnp.int32, (8, orders), 0) < 4, sine, -sine)

    for copy in copies:
        copy.wait()
    packed = packed_ref[...]
    for d in range(1, group):
        packed = packed + recv1[d - 1]
    parts = [jnp.where(rep == r, packed, 0.0) for r in range(16)]
    vectors = dot(
        jnp.concatenate(parts, axis=0).astype(jnp.bfloat16), spread_matrix()
    ).astype(jnp.bfloat16)
    for l in range(degrees):
        y_ref[l * width : (l + 1) * width, :] = dot(
            fo_ref[l], vectors[l * width : (l + 1) * width]
        )
    for q in range(q_orders):
        for part, z in enumerate(axial_result(dot(ao_ref[q], axial_operand(y_ref, q)))):
            start = (q * 2 + part) * nloc
            zq_ref[start : start + nloc, :] = z

    for block in range(nloc // 8):
        gathered = jnp.zeros((QP, 128), jnp.float32)
        for n8 in range(8):
            n = block * 8 + n8
            real = zq_ref[pl.ds(n, QP, stride=2 * nloc), :]
            imag = zq_ref[pl.ds(nloc + n, QP, stride=2 * nloc), :]
            both = jnp.where(rep % 2 == 0, real, imag)
            gathered = jnp.where(rep // 2 == n8, both, gathered)
        flipped = gathered.T
        for n8 in range(8):
            n = block * 8 + n8
            framed = jnp.concatenate(
                [flipped[n8 * 8 : n8 * 8 + 8], flipped[64 + n8 * 8 : 72 + n8 * 8]], axis=0
            ).astype(jnp.bfloat16)
            values = dot(framed, turn_ref[n])
            for u in range(2):
                v = values[u * 8 : u * 8 + 8]
                vals_ref[n, u * 8 : u * 8 + 8, :] = cosine * v + sine * pltpu.roll(v, 4, 0)

    half = nloc // 2
    for m in range(orders // 128):
        cols = slice(m * 128, (m + 1) * 128)
        for n in range(half):
            a = vals_ref[n, :, cols]
            b = vals_ref[n + half, :, cols]
            rows = slice(n * 16, (n + 1) * 16)
            sbuf[2 * m, rows, :] = jnp.where(low, a, pltpu.roll(b, 64, 1)).astype(jnp.bfloat16)
            sbuf[2 * m + 1, rows, :] = jnp.where(low, pltpu.roll(a, 64, 1), b).astype(
                jnp.bfloat16
            )

    copies = []
    for d in range(1, leaf_size):
        to_leaf = lax.rem(my_leaf + d, leaf_size)
        copy = pltpu.make_async_remote_copy(
            src_ref=sbuf.at[to_leaf],
            dst_ref=recv2.at[d - 1],
            send_sem=send2.at[d - 1],
            recv_sem=rsem2.at[d - 1],
            device_id=device(to_leaf * group + my_g),
            device_id_type=MESH,
        )
        copy.start()
        copies.append(copy)
    make_tables(tab_c, tab_s)
    for copy in copies:
        copy.wait()
    root = sbuf[my_leaf].astype(jnp.float32)
    for d in range(1, leaf_size):
        root = root + recv2[d - 1].astype(jnp.float32)
    root_ref[...] = root.astype(jnp.bfloat16).astype(jnp.float32)

    lats = ang_ref.shape[1] // 2
    sign = jnp.where(lax.broadcasted_iota(jnp.int32, (8, 128), 0) < 4, -1.0, 1.0)

    def field_copy(d):
        target = lax.rem(me + d, holders)
        return pltpu.make_async_remote_copy(
            src_ref=fbuf.at[target],
            dst_ref=recv3.at[me],
            send_sem=send3.at[d - 1],
            recv_sem=rsem3.at[d - 1],
            device_id=device(target),
            device_id_type=MESH,
        )

    def latitude(h):
        theta = jnp.zeros((8, 128), jnp.float32)
        cross = jnp.zeros((8, 128), jnp.float32)
        for n in range(half):
            a0 = ang_ref[n, pl.ds(h, 1), :]
            a1 = ang_ref[n, pl.ds(lats + h, 1), :]
            r0 = root_ref[n * 16 : n * 16 + 8, :]
            r1 = root_ref[n * 16 + 8 : n * 16 + 16, :]
            theta = theta + (a0 * r0 + a1 * r1)
            cross = cross + (a1 * r0 + a0 * r1)
        theta = theta + pltpu.roll(theta, 64, 1)
        cross = cross + pltpu.roll(cross, 64, 1)
        phi = sign * pltpu.roll(cross, 4, 0)
        fbuf[h] = jnp.concatenate([theta, phi], axis=0).astype(jnp.bfloat16)

    def start(d, carry):
        latitude(lax.rem(me + d, holders))
        field_copy(d).start()
        return carry

    def finish(d, carry):
        field_copy(d).wait_send()
        source = lax.rem(me + holders - d, holders)
        pltpu.make_async_remote_copy(
            src_ref=fbuf.at[source],
            dst_ref=recv3.at[source],
            send_sem=send3.at[d - 1],
            recv_sem=rsem3.at[d - 1],
            device_id=device(source),
            device_id_type=MESH,
        ).wait_recv()
        return carry

    lax.fori_loop(1, holders, start, 0)
    latitude(me)
    recv3[me] = fbuf[me]
    lax.fori_loop(1, holders, finish, 0)

    pieces = []
    for leaf in range(leaf_size):
        total = recv3[leaf * group].astype(jnp.float32)
        for g in range(1, group):
            total = total + recv3[leaf * group + g].astype(jnp.float32)
        pieces.append(total)
    spectrum = jnp.concatenate(
        [
            jnp.where(low, pieces[2 * m], pieces[2 * m + 1]).astype(jnp.bfloat16)
            for m in range(leaf_size // 2)
        ],
        axis=1,
    )
    scale = 1.0 / math.sqrt(orders)
    for tile in range(PHI // 512):
        cols = slice(tile * 512, (tile + 1) * 512)
        first = dot(spectrum, tab_c[:, cols])
        second = dot(spectrum, tab_s[:, cols])
        for c in range(2):
            rows = slice(c * 8, c * 8 + 8)
            turned = pltpu.roll(second[rows], 4, 0)
            out_ref[rows, cols] = (first[rows] + jnp.tile(sign, (1, 4)) * turned) * scale


def pad_last(x, *sizes):
    skip = x.ndim - len(sizes)
    return jnp.pad(
        x, [(0, 0)] * skip + [(0, s - n) for s, n in zip(sizes, x.shape[skip:], strict=True)]
    )


def rotation_blocks(real, imag):
    real = pad_last(real.astype(jnp.bfloat16), QP, QP)
    imag = pad_last(imag.astype(jnp.bfloat16), QP, QP)
    return jnp.concatenate(
        [jnp.concatenate([real, -imag], -1), jnp.concatenate([imag, real], -1)], -2
    )


def axial_rows(mats):
    mats = mats.reshape(-1, mats.shape[-1])
    return jnp.pad(mats, ((0, 16), (0, 128 - mats.shape[1])))


def on_device(
    dims,
    sphere_coef,
    live_blocks,
    cluster,
    leaf_parent,
    leaf_octant,
    box_octant,
    rotation,
    axial_one,
    axial_two,
    owner_rotation,
    owner_axial,
    owner_angle,
    turn_table,
    angular_table,
):
    leaf_size, state_size, sub_size = dims
    group = state_size * sub_size
    holders = leaf_size * group
    degrees, morders = sphere_coef.shape[:2]
    slots = sphere_coef.shape[-1]
    bf16 = jnp.bfloat16
    f32 = jnp.float32

    xs = sphere_coef.reshape(-1, slots)
    w = jnp.transpose(rotation, (0, 2, 3, 1, 4)).reshape(-1, morders)
    w = jnp.pad(w, ((0, 16), (0, 128 - morders)))
    s1 = axial_rows(jnp.transpose(axial_one, (0, 2, 3, 5, 4, 1)))
    s2 = axial_rows(jnp.transpose(axial_two, (0, 2, 3, 5, 4, 1)))
    rows = degrees * 2 * QP
    vmem = pl.BlockSpec(memory_space=pltpu.VMEM)
    packed = pl.pallas_call(
        functools.partial(local_kernel, morders),
        out_shape=jax.ShapeDtypeStruct((rows // 16, 128), f32),
        in_specs=[pl.BlockSpec(memory_space=pltpu.SMEM)] * 4 + [vmem] * 5,
        out_specs=vmem,
        scratch_shapes=[
            pltpu.VMEM((rows, 128), bf16),
            pltpu.VMEM((LP * 2 * QP, 128), f32),
            pltpu.VMEM((LP * 2 * QP, 128), f32),
            pltpu.VMEM((QP * 2 * LP, 128), f32),
            pltpu.VMEM((QP * 2 * LP, 128), f32),
            pltpu.VMEM((degrees, 8, 2 * QP, 128), bf16),
        ],
        compiler_params=pltpu.CompilerParams(vmem_limit_bytes=32 * 1024 * 1024),
    )(
        box_octant,
        live_blocks,
        leaf_octant,
        leaf_parent,
        xs,
        cluster.reshape(1, slots),
        w,
        s1,
        s2,
    )

    fo = rotation_blocks(owner_rotation[0, 0], owner_rotation[0, 1])
    nloc = turn_table.shape[1]
    orders = turn_table.shape[3]
    so = axial_rows(jnp.transpose(owner_axial[0], (0, 1, 2, 5, 4, 3)))
    turn = pad_last(turn_table[0], QP, orders)
    own = angular_table.shape[0]
    ang = jnp.transpose(angular_table, (1, 2, 0)).reshape(2, nloc // 2, -1, own)
    ang = jnp.concatenate([ang[0], ang[1]], axis=-1).astype(f32)
    lats = ang.shape[1] // 2
    assert own == 64 and lats == holders and orders == 64 * leaf_size

    out = pl.pallas_call(
        functools.partial(owner_kernel, dims),
        out_shape=jax.ShapeDtypeStruct((16, PHI), f32),
        in_specs=[vmem] * 3 + [pl.BlockSpec(memory_space=pltpu.SMEM)] + [vmem] * 2,
        out_specs=vmem,
        scratch_shapes=[
            pltpu.VMEM((group - 1, rows // 16, 128), f32),
            pltpu.VMEM((morders, 2 * nloc, 64), bf16),
            pltpu.VMEM((LP * 2 * QP, 128), f32),
            pltpu.VMEM((QP * 2 * nloc, 128), f32),
            pltpu.VMEM((nloc, 16, orders), f32),
            pltpu.VMEM((leaf_size, 8 * nloc, 128), bf16),
            pltpu.VMEM((leaf_size - 1, 8 * nloc, 128), bf16),
            pltpu.VMEM((8 * nloc, 128), f32),
            pltpu.VMEM((lats, 16, 128), bf16),
            pltpu.VMEM((holders, 16, 128), bf16),
            pltpu.VMEM((orders, PHI), bf16),
            pltpu.VMEM((orders, PHI), bf16),
            pltpu.SemaphoreType.DMA((group - 1,)),
            pltpu.SemaphoreType.DMA((group - 1,)),
            pltpu.SemaphoreType.DMA((leaf_size - 1,)),
            pltpu.SemaphoreType.DMA((leaf_size - 1,)),
            pltpu.SemaphoreType.DMA((holders - 1,)),
            pltpu.SemaphoreType.DMA((holders - 1,)),
        ],
        compiler_params=pltpu.CompilerParams(
            collective_id=0, has_side_effects=True, vmem_limit_bytes=48 * 1024 * 1024
        ),
    )(packed, fo, so, owner_angle, turn, ang)
    out = out.reshape(2, 2, 4, PHI)
    return jnp.transpose(out, (2, 0, 1, 3))[None]


def solution(mesh):
    dims = (mesh.shape["leaf"], mesh.shape["state"], mesh.shape["sub"])
    split = ("groups", "leaf", "state", "sub")
    return jax.shard_map(
        functools.partial(on_device, dims),
        mesh=mesh,
        in_specs=(
            P(None, None, None, None, None, split),
            P(split),
            P(split),
            P(split),
            P(split),
            P(split),
            P(),
            P(),
            P(),
            P(("groups", "leaf"), None, None, None, None),
            P(("groups", "leaf"), None, None, None, ("state", "sub"), None, None),
            P("groups"),
            P(("groups", "leaf"), ("state", "sub"), None, None),
            P("leaf", ("state", "sub"), None),
        ),
        out_specs=P(split, None, None, None, None),
        check_vma=False,
    )
```
